512 devices in a mesh: grp: 16 (over y, x), tile: 32 (over z, core).
Axes of the slice: x: 4, y: 4, z: 16, core: 2. Of those that a mesh axis runs over, the one named last changes fastest.
Arguments:
- latent: bfloat16 [8, 64, 64, 512], P(None, 'grp', 'tile'), may hold values from -36 to 36
- coarse_filters: bfloat16 [3, 3, 3, 512, 512], P(None, None, None, None, 'grp'), may hold values from -0.0546875 to 0.0546875
- mid_filters: bfloat16 [3, 3, 3, 256, 256], P(None, None, None, None, 'tile'), may hold values from -0.078125 to 0.078125
- fine_filters: bfloat16 [3, 3, 3, 128, 128], replicated, may hold values from -0.109375 to 0.109375
- coarse_proj: bfloat16 [512, 256], replicated, may hold values from -0.25 to 0.25
- mid_proj: bfloat16 [256, 128], replicated, may hold values from -0.375 to 0.375
Outputs:
- frames_out: bfloat16 [8, 256, 256, 128], P(None, 'grp', 'tile')
The draws below stay inside these ranges and needn't reach their ends.
All inputs are finite; a program needn't handle non-finite values.
Results may differ from the reference program's by a relative error of at most 0.018.
Values may be sent and summed in bfloat16 or wider, within the bound.
A program may use at most 128 MiB of HBM per device.

```python
import math
import jax
import jax.numpy as jnp
from jax import lax

C0 = 512
C1 = 256
C2 = 128
FRAMES = 8
H0 = 64
W0 = 64


def draw_latent(key, part):
    keys = jax.random.split(key, 3)
    shape = (FRAMES, H0, W0, C0)
    cell_scale = jnp.exp(jax.random.uniform(keys[0], (FRAMES, H0, W0, 1), jnp.float32, math.log(0.3), math.log(3.0)))
    chan_scale = jnp.exp(jax.random.uniform(keys[1], (1, 1, 1, C0), jnp.float32, math.log(0.3), math.log(3.0)))
    base = jax.random.normal(keys[2], shape, jnp.float32)
    base = jnp.clip(base, -4.0, 4.0)
    return (base * cell_scale * chan_scale).astype(jnp.bfloat16)


def block_scale(own_key, extent, pieces, least, largest):
    level, own = 1.0, jax.random.fold_in(own_key, 6)
    for axis_at, parts in pieces:
        draws = jnp.exp(jax.random.uniform(jax.random.fold_in(own, axis_at), (parts,), jnp.float32, least / len(pieces), largest / len(pieces)))
        level = level * jnp.repeat(draws, extent[axis_at] // parts).reshape([-1 if axis == axis_at else 1 for axis in range(len(extent))])
    return level


def gaussian(stream_key, extent, deviation, limit, shards=(), dtype=jnp.bfloat16):
    drawn = deviation * jax.random.normal(stream_key, extent, jnp.float32)
    if shards:
        drawn = drawn * block_scale(stream_key, extent, shards, -0.22, 0.18)
    return jnp.clip(drawn, -limit, limit).astype(dtype)


def setup_inputs(seed: int = 0) -> dict:
    streams_of = jax.random.split(jax.random.key(seed), 7)
    return {
        "latent": draw_latent(jax.random.fold_in(streams_of[6], 71), 0),
        "coarse_filters": gaussian(streams_of[1], (3, 3, 3, C0, C0), (27 * C0) ** -0.5, 0.0546875, ((4, 16),)),
        "mid_filters": gaussian(streams_of[2], (3, 3, 3, C1, C1), (27 * C1) ** -0.5, 0.078125, ((4, 32),)),
        "fine_filters": gaussian(streams_of[3], (3, 3, 3, C2, C2), (27 * C2) ** -0.5, 0.109375),
        "coarse_proj": gaussian(streams_of[4], (C0, C1), C0 ** -0.5, 0.25),
        "mid_proj": gaussian(streams_of[5], (C1, C2), C1 ** -0.5, 0.375),
    }


def activate(values):
    widened = values.astype(jnp.float32)
    scaled = widened * lax.rsqrt(lax.optimization_barrier(jnp.mean(widened * widened, axis=-1, keepdims=True)) + 1e-06)
    return jax.nn.silu(scaled).astype(jnp.bfloat16)

def double_size(values):
    return jnp.repeat(jnp.repeat(values, 2, axis=1), 2, axis=2)

def causal_conv(values, filters):
    result = lax.conv_general_dilated(values[None], filters, window_strides=(1, 1, 1), padding=((2, 0), (1, 1), (1, 1)), dimension_numbers=('NDHWC', 'DHWIO', 'NDHWC'), preferred_element_type=jnp.float32)
    return result[0]

def reference(latent, coarse_filters, mid_filters, fine_filters, coarse_proj, mid_proj):
    coarse_out = causal_conv(activate(latent), coarse_filters).astype(jnp.bfloat16)
    level_zero = (latent.astype(jnp.float32) + coarse_out.astype(jnp.float32)).astype(jnp.bfloat16)
    reduced = jnp.dot(level_zero, coarse_proj, preferred_element_type=jnp.float32).astype(jnp.bfloat16)
    mid_act = double_size(activate(reduced))
    mid_out = (double_size(reduced).astype(jnp.float32) + causal_conv(mid_act, mid_filters)).astype(jnp.bfloat16)
    fine_low = jnp.dot(mid_out, mid_proj, preferred_element_type=jnp.float32).astype(jnp.bfloat16)
    fine_act = double_size(activate(fine_low))
    return (double_size(fine_low).astype(jnp.float32) + causal_conv(fine_act, fine_filters)).astype(jnp.bfloat16)
```

```python
import jax
import jax.numpy as jnp
from jax import lax
from jax.experimental import pallas as pl
from jax.experimental.pallas import tpu as pltpu
from jax.sharding import PartitionSpec as P

MESH = pl.DeviceIdType.MESH
F32 = jnp.float32
BF16 = jnp.bfloat16
NY = 4
NX = 4
NG = 16
NT_DIMS = (((1,), (1,)), ((), ()))
NN_DIMS = (((1,), (0,)), ((), ()))
SHIFTS = ((-1, 0, 0), (0, 0, 1))


def activate(values):
    scaled = values * lax.rsqrt(jnp.mean(values * values, axis=-1, keepdims=True) + 1e-06)
    return scaled / (1.0 + jnp.exp(-scaled))


def lane_group(rows):
    return lax.broadcasted_iota(jnp.int32, (rows, 128), 1) // 32


def pack_four(parts):
    group = lane_group(8)
    frame = lax.broadcasted_iota(jnp.int32, (8, 128), 0)
    one_back = (group == 1) & (frame >= 1)
    two_back = (group == 2) & (frame >= 2)
    total = None
    for k in range(4):
        mixed = jnp.where(
            group == 0, parts[k], jnp.where(group == 1, parts[(k + 1) % 4], parts[(k + 2) % 4])
        )
        moved = jnp.where(
            group == 0,
            mixed,
            jnp.where(
                one_back,
                pltpu.roll(mixed, 1, 0),
                jnp.where(two_back, pltpu.roll(mixed, 2, 0), 0.0),
            ),
        )
        turned = pltpu.roll(moved, 32 * k, 1) if k else moved
        total = turned if total is None else total + turned
    return total


def swap_groups(parts):
    rows = parts[0].shape[0]
    group = lane_group(rows)

    def pick(options):
        return jnp.where(
            group == 0,
            options[0],
            jnp.where(group == 1, options[1], jnp.where(group == 2, options[2], options[3])),
        )

    turned = []
    for k in range(4):
        mixed = pick([parts[(q + k) % 4] for q in range(4)])
        turned.append(pltpu.roll(mixed, 32 * k, 1) if k else mixed)
    return [pick([turned[(p - i) % 4] for p in range(4)]) for i in range(4)]


def frames_back(values, steps):
    frame = lax.broadcasted_iota(jnp.int32, values.shape, 1)
    return jnp.where(frame >= steps, pltpu.roll(values, steps, 1), 0.0)


def make_kernel(nz):
    nt = 2 * nz
    outs = 256 // nt
    half_ring = nz // 2

    def kernel(
        latent, cw_hbm, mw, fw_hbm, cproj, mproj, out,
        lat, gath, cw, prod, edge_out, edge_in, main, a2a_out, a2a_in,
        mine, theirs, wm, level, mact, mcol, mcor, mrow_in, mcol_in, mcor_in,
        mx3, mprod, fw, flow, fx, frow, fcol, fcor, frow_in, fcol_in, fcor_in, fprod, result,
        local_sem, send_sem, g1_sem, g2_sem, sib_sem, ring_sem, share_sem,
        edge_sem, a2a_sem, mh_sem, fh_sem,
    ):
        g = lax.axis_index("grp")
        t = lax.axis_index("tile")
        y, x = g // NX, g % NX
        z, core = t // 2, t % 2
        up_g, down_g = (g + NG - 1) % NG, (g + 1) % NG
        left_t, right_t = (t + nt - 1) % nt, (t + 1) % nt
        sib_t = z * 2 + 1 - core

        def gid(yy, xx):
            return ((yy + NY) % NY) * NX + (xx + NX) % NX

        def ring_t(dz):
            return ((z + dz + nz) % nz) * 2 + core

        sent = []

        def remote(src, dst, sem, dev):
            return pltpu.make_async_remote_copy(
                src_ref=src, dst_ref=dst, send_sem=send_sem.at[len(sent)], recv_sem=sem,
                device_id=dev, device_id_type=MESH,
            )

        def send(src, dst, sem, dev):
            copy = remote(src, dst, sem, dev)
            copy.start()
            sent.append(copy)

        def arrived(dst, sem):
            pltpu.make_async_remote_copy(
                src_ref=dst, dst_ref=dst, send_sem=send_sem.at[0], recv_sem=sem,
                device_id=(g, left_t), device_id_type=MESH,
            ).wait_recv()

        barrier = pltpu.get_barrier_semaphore()
        partners = [((g + d) % NG, t) for d in range(1, NG)]
        partners += [(g, left_t), (g, right_t), (g, ring_t(1)), (g, ring_t(-1))]
        partners += [(a, b) for a in (up_g, down_g) for b in (left_t, right_t)]
        for dev in partners:
            pl.semaphore_signal(barrier, inc=1, device_id=dev, device_id_type=MESH)

        locals_ = []
        for a in range(3):
            locals_.append(
                pltpu.make_async_copy(
                    cw_hbm.at[a], cw.at[:, pl.ds(32 * (2 - a), 32), :], local_sem.at[a]
                )
            )
            locals_.append(
                pltpu.make_async_copy(
                    fw_hbm.at[a], fw.at[:, pl.ds(128 * a, 128), :], local_sem.at[3 + a]
                )
            )
        for copy in locals_:
            copy.start()

        for f in range(8):
            cells = latent[f].astype(F32).reshape(8, 512)
            for big in range(4):
                lat[big, pl.ds(8 * f, 8), :] = cells[:, 128 * big : 128 * big + 128]

        def lat_cell(big, cell):
            return lat[big, pl.ds(cell, 8, stride=8), :]

        own_lat = jnp.concatenate(
            [
                jnp.concatenate([lat_cell(big, cell) for big in range(4)], axis=1)
                for cell in range(8)
            ],
            axis=0,
        )
        gath[g] = activate(own_lat).astype(BF16)
        own_mw = jnp.concatenate(
            [mw[...].astype(F32), jnp.zeros((1, outs, 256), F32)], axis=0
        )
        mine[...] = own_mw.reshape(28 * outs, 256).astype(BF16)
        cw[:, pl.ds(96, 32), :] = jnp.zeros((9, 32, 512), BF16)
        prod[:, 0] = jnp.zeros((9, 16, 128), F32)
        prod[:, 65] = jnp.zeros((9, 16, 128), F32)

        pl.semaphore_wait(barrier, len(partners))

        def near(h, axis, d):
            along_x = (axis == 1) == (h == 0)
            return (gid(y, x + d), t) if along_x else (gid(y + d, x), t)

        def shard(h, d1, d2):
            return gid(y + d2, x + d1) if h == 0 else gid(y + d1, x + d2)

        def part(h, d1, d2, first, count):
            return gath.at[shard(h, d1, d2), pl.ds(32 * h + first, count), :]

        steps = (0, -1, 1, 2)

        def second(h, k):
            src = part(h, steps[k], 0, 0, 32)
            send(src, src, g2_sem.at[h, k, 0], near(h, 2, 1))
            send(src, src, g2_sem.at[h, k, 1], near(h, 2, -1))

        def pass_on(h, k):
            arrived(part(h, steps[k], -1, 0, 32), g2_sem.at[h, k, 0])
            src = part(h, steps[k], -1, 0, 16)
            send(src, src, g2_sem.at[h, k, 2], near(h, 2, 1))
            arrived(part(h, steps[k], 1, 0, 32), g2_sem.at[h, k, 1])
            src = part(h, steps[k], 1, 16, 16)
            send(src, src, g2_sem.at[h, k, 3], near(h, 2, -1))

        for h in range(2):
            src = part(h, 0, 0, 0, 32)
            send(src, src, g1_sem.at[h, 0], near(h, 1, 1))
            send(src, src, g1_sem.at[h, 1], near(h, 1, -1))
        send(mine, theirs, sib_sem.at[0], (g, sib_t))
        for h in range(2):
            second(h, 0)

        arrived(theirs, sib_sem.at[0])
        own_f = mine[...].astype(F32).reshape(28, outs, 256)
        other_f = theirs[...].astype(F32).reshape(28, outs, 256)
        even = (jnp.zeros((1, 1, 256), jnp.int32) + core) == 0
        joined = jnp.concatenate(
            [jnp.where(even, own_f, other_f), jnp.where(even, other_f, own_f)], axis=1
        )
        rows_z = pl.multiple_of(2 * outs * z, 16)
        for a in range(3):
            for qh in range(2):
                wm[:, pl.ds(rows_z, 2 * outs), pl.ds(384 * qh + 128 * a, 128)] = joined[
                    9 * a : 9 * a + 9, :, 128 * qh : 128 * qh + 128
                ].astype(BF16)

        def block(dz):
            row = pl.multiple_of(2 * outs * ((z + dz + nz) % nz), 16)
            lane = pl.multiple_of(384 * core, 128)
            return wm.at[:, pl.ds(row, 2 * outs), pl.ds(lane, 384)]

        def sib_block(dz):
            row = pl.multiple_of(2 * outs * ((z + dz + nz) % nz), 16)
            lane = pl.multiple_of(384 * (1 - core), 128)
            return wm.at[:, pl.ds(row, 2 * outs), pl.ds(lane, 384)]

        sign = 1 - 2 * core

        def ring_send(k):
            if k < half_ring:
                send(block(1 - k), block(1 - k), ring_sem.at[0, k], (g, ring_t(1)))
                send(block(k - 1), block(k - 1), ring_sem.at[1, k], (g, ring_t(-1)))
            elif k == half_ring:
                src = block(-sign * (k - 1))
                send(src, src, ring_sem.at[0, k], (g, ring_t(sign)))

        def share(dz, slot):
            send(block(dz), block(dz), share_sem.at[slot], (g, sib_t))

        def ring_step(k):
            if k < half_ring:
                arrived(block(-k), ring_sem.at[0, k])
                arrived(block(k), ring_sem.at[1, k])
                ring_send(k + 1)
                share(-k, 2 * k)
                share(k, 2 * k + 1)
            elif k == half_ring:
                arrived(block(k), ring_sem.at[0, k])
                share(k, 2 * k)

        ring_send(1)

        for h in range(2):
            arrived(part(h, -1, 0, 0, 32), g1_sem.at[h, 0])
            src = part(h, -1, 0, 0, 16)
            send(src, src, g1_sem.at[h, 2], near(h, 1, 1))
            arrived(part(h, 1, 0, 0, 32), g1_sem.at[h, 1])
            src = part(h, 1, 0, 16, 16)
            send(src, src, g1_sem.at[h, 3], near(h, 1, -1))
        for h in range(2):
            second(h, 1)
            second(h, 2)
        for h in range(2):
            pass_on(h, 0)
        for h in range(2):
            arrived(part(h, 2, 0, 0, 16), g1_sem.at[h, 2])
            arrived(part(h, 2, 0, 16, 16), g1_sem.at[h, 3])
            second(h, 3)
        ring_step(1)
        for k in (1, 2):
            for h in range(2):
                pass_on(h, k)
        for h in range(2):
            pass_on(h, 3)
        ring_step(2)
        for h in range(2):
            for k in range(4):
                arrived(part(h, steps[k], 2, 0, 16), g2_sem.at[h, k, 2])
                arrived(part(h, steps[k], 2, 16, 16), g2_sem.at[h, k, 3])
        for copy in locals_:
            copy.wait()

        def coarse_rows(q, _):
            acts = gath[pl.ds(4 * q, 4)].reshape(256, 512)
            for b in range(3):
                found = lax.dot_general(
                    acts, cw[pl.ds(3 * b, 3)].reshape(384, 512), NT_DIMS,
                    preferred_element_type=F32,
                )
                for c in range(3):
                    prod[3 * b + c, pl.ds(16 * q + 1, 16)] = found[
                        :, 128 * c : 128 * c + 128
                    ].reshape(16, 16, 128)
            return 0

        lax.fori_loop(0, 2, coarse_rows, 0)
        ring_step(3)
        lax.fori_loop(2, 4, coarse_rows, 0)

        def taps(row, c, j):
            return sum(prod[3 * b + c, row + b, pl.ds(8 * j, 8), :] for b in range(3))

        def edges(rr, _):
            for e, (c, j) in enumerate(((2, 0), (0, 1))):
                both = [
                    pack_four([taps(8 * rr + 4 * s + i, c, j) for i in range(4)]) for s in range(2)
                ]
                edge_out[e, rr] = jnp.concatenate(both, axis=0).astype(BF16)
            return 0

        lax.fori_loop(0, 8, edges, 0)
        send(edge_out.at[0], edge_in.at[1], edge_sem.at[1], (g, left_t))
        send(edge_out.at[1], edge_in.at[0], edge_sem.at[0], (g, right_t))

        def mains(r, _):
            for j in range(2):
                main[r, pl.ds(8 * j, 8), :] = pack_four(
                    [
                        taps(4 * r + i, 1, j) + taps(4 * r + i, 2 if j == 0 else 0, 1 - j)
                        for i in range(4)
                    ]
                )
            return 0

        lax.fori_loop(0, 16, mains, 0)
        ring_step(4)

        def inside(condition, like):
            return (jnp.zeros(like, jnp.int32) + condition.astype(jnp.int32)) > 0

        has_left, has_right = t > 0, t < nt - 1
        has_up, has_down = g > 0, g < NG - 1

        for j, has in ((0, has_left), (1, has_right)):
            arrived(edge_in.at[j], edge_sem.at[j])
            added = edge_in[j].astype(F32).reshape(16, 8, 128)
            added = jnp.where(inside(has, (16, 8, 128)), added, 0.0)
            main[:, pl.ds(8 * j, 8), :] = main[:, pl.ds(8 * j, 8), :] + added
        a2a_out[...] = main[...].astype(BF16)

        for d in range(1, NG):
            r = (g + d) % NG
            send(a2a_out.at[r], a2a_in.at[g], a2a_sem.at[d], (r, t))
        a2a_in[g] = a2a_out[g]
        ring_step(5)
        for d in range(1, NG):
            arrived(a2a_in.at[(g + NG - d) % NG], a2a_sem.at[d])

        for big in range(4):
            found = swap_groups([a2a_in[4 * big + p].astype(F32) for p in range(4)])
            for i in range(4):
                cells = jnp.concatenate(
                    [
                        lat_cell(big, 2 * i + j)
                        for j in range(2)
                    ],
                    axis=0,
                )
                level[pl.ds(16 * i, 16), pl.ds(128 * big, 128)] = (cells + found[i]).astype(BF16)
        reduced = jnp.dot(level[...], cproj[...], preferred_element_type=F32)
        reduced = reduced.astype(BF16).astype(F32)
        act = activate(reduced)
        mact[...] = act.astype(BF16)
        cells = act.reshape(8, 8, 256)
        for j in range(2):
            mcol[j] = jnp.concatenate(
                [act[16 * i + 8 * j : 16 * i + 8 * j + 8] for i in range(4)], axis=0
            ).astype(BF16)
            for i in range(2):
                corner = cells[6 * i + j]
                mcor[2 * i + j] = jnp.concatenate([corner, corner], axis=0).astype(BF16)

        def halo(row_first, row_last, col, cor, row_in, col_in, cor_in, sem):
            send(col.at[0], col_in.at[1], sem.at[3], (g, left_t))
            send(col.at[1], col_in.at[0], sem.at[2], (g, right_t))
            send(row_first, row_in.at[1], sem.at[1], (up_g, t))
            send(row_last, row_in.at[0], sem.at[0], (down_g, t))
            send(cor.at[0], cor_in.at[3], sem.at[7], (up_g, left_t))
            send(cor.at[1], cor_in.at[2], sem.at[6], (up_g, right_t))
            send(cor.at[2], cor_in.at[1], sem.at[5], (down_g, left_t))
            send(cor.at[3], cor_in.at[0], sem.at[4], (down_g, right_t))

        def halo_wait(row_in, col_in, cor_in, sem):
            for i in range(2):
                arrived(row_in.at[i], sem.at[i])
                arrived(col_in.at[i], sem.at[2 + i])
            for i in range(4):
                arrived(cor_in.at[i], sem.at[4 + i])

        halo(
            mact.at[pl.ds(0, 16)], mact.at[pl.ds(48, 16)], mcol, mcor,
            mrow_in, mcol_in, mcor_in, mh_sem,
        )
        for k in range(6, half_ring + 1):
            ring_step(k)
        halo_wait(mrow_in, mcol_in, mcor_in, mh_sem)

        def surround(center, row_in, col_in, cor_in, height, breadth):
            lanes = row_in.shape[-1]

            def keep(values, *conditions):
                for condition in conditions:
                    values = jnp.where(inside(condition, values.shape), values, 0.0)
                return values

            above = keep(row_in[0].astype(F32), has_up).reshape(breadth, 8, lanes)
            below = keep(row_in[1].astype(F32), has_down).reshape(breadth, 8, lanes)
            left = keep(col_in[0].astype(F32), has_left).reshape(height, 8, lanes)
            right = keep(col_in[1].astype(F32), has_right).reshape(height, 8, lanes)
            corner = [
                keep(cor_in[2 * i + j].astype(F32)[0:8], (has_up, has_down)[i], (has_left, has_right)[j])
                for i in range(2)
                for j in range(2)
            ]
            tiles = [corner[0]] + [above[j] for j in range(breadth)] + [corner[1]]
            for i in range(height):
                tiles += [left[i]] + [center(i, j) for j in range(breadth)] + [right[i]]
            tiles += [corner[2]] + [below[j] for j in range(breadth)] + [corner[3]]
            return jnp.concatenate([tile[None] for tile in tiles], axis=0)

        around = surround(
            lambda i, j: cells[2 * i + j], mrow_in, mcol_in, mcor_in, 4, 2
        )
        for a in range(3):
            moved = frames_back(around, 2 - a) if a < 2 else around
            moved = moved.reshape(192, 256).astype(BF16)
            for qh in range(2):
                mx3[:, pl.ds(384 * qh + 128 * a, 128)] = moved[:, 128 * qh : 128 * qh + 128]

        for k in range(1, half_ring):
            arrived(sib_block(-k), share_sem.at[2 * k])
            arrived(sib_block(k), share_sem.at[2 * k + 1])
        arrived(sib_block(half_ring), share_sem.at[2 * half_ring])

        def mid_tap(bc, _):
            mprod[bc] = lax.dot_general(
                mx3[...], wm[bc], NT_DIMS, preferred_element_type=F32
            ).reshape(6, 4, 8, 256)
            return 0

        lax.fori_loop(0, 9, mid_tap, 0)

        def upsampled(products, height, breadth, pr, pc, residual):
            total = residual
            for b in range(3):
                low = 1 + SHIFTS[pr][b]
                for c in range(3):
                    side = 1 + SHIFTS[pc][c]
                    total = total + products[
                        3 * b + c, pl.ds(low, height), pl.ds(side, breadth)
                    ]
            return total

        residual = reduced.reshape(4, 2, 8, 256)
        for pr in range(2):
            for pc in range(2):
                middle = upsampled(mprod, 4, 2, pr, pc, residual).astype(BF16).reshape(64, 256)
                low = jnp.dot(middle, mproj[...], preferred_element_type=F32)
                low = low.astype(BF16).astype(F32)
                lively = activate(low)
                for i in range(4):
                    for j in range(2):
                        at = 16 * i + 8 * j
                        flow[2 * i + pr, 2 * j + pc] = low[at : at + 8]
                        fx[2 * i + pr, 2 * j + pc] = lively[at : at + 8]

        frow[0] = fx[0].reshape(32, 128).astype(BF16)
        frow[1] = fx[7].reshape(32, 128).astype(BF16)
        fcol[0] = fx[:, 0].reshape(64, 128).astype(BF16)
        fcol[1] = fx[:, 3].reshape(64, 128).astype(BF16)
        for i in range(2):
            for j in range(2):
                corner = fx[7 * i, 3 * j]
                fcor[2 * i + j] = jnp.concatenate([corner, corner], axis=0).astype(BF16)
        halo(frow.at[0], frow.at[1], fcol, fcor, frow_in, fcol_in, fcor_in, fh_sem)
        halo_wait(frow_in, fcol_in, fcor_in, fh_sem)

        around = surround(lambda i, j: fx[i, j], frow_in, fcol_in, fcor_in, 8, 4)
        fine = jnp.concatenate(
            [
                (frames_back(around, 2 - a) if a < 2 else around).reshape(480, 128).astype(BF16)
                for a in range(3)
            ],
            axis=1,
        )
        for pair in range(5):
            names = [bc for bc in (2 * pair, 2 * pair + 1) if bc < 9]
            filters = jnp.concatenate([fw[bc] for bc in names], axis=1)
            found = lax.dot_general(fine, filters, NN_DIMS, preferred_element_type=F32)
            for n, bc in enumerate(names):
                fprod[bc] = found[:, 128 * n : 128 * n + 128].reshape(10, 6, 8, 128)

        for pr in range(2):
            for pc in range(2):
                for i in range(8):
                    for j in range(4):
                        total = flow[i, j]
                        for b in range(3):
                            for c in range(3):
                                total = total + fprod[
                                    3 * b + c, i + 1 + SHIFTS[pr][b], j + 1 + SHIFTS[pc][c]
                                ]
                        spot = 8 * (2 * i + pr) + 2 * j + pc
                        result[pl.ds(spot, 8, stride=128), :] = total
        out[...] = result[...].astype(BF16).reshape(8, 16, 8, 128)

        for copy in sent:
            copy.wait_send()

    return kernel


def count_sends(nz):
    ring = 2 * (nz // 2 - 1) + 1
    return 8 + 32 + 1 + 2 * ring + 2 + 15 + 16


def body(latent, coarse_filters, mid_filters, fine_filters, coarse_proj, mid_proj):
    nz = lax.axis_size("tile") // 2
    outs = mid_filters.shape[4]
    cw = jnp.transpose(coarse_filters, (0, 1, 2, 4, 3)).reshape(3, 9, 32, 512)
    mw = jnp.transpose(mid_filters, (0, 1, 2, 4, 3)).reshape(27, outs, 256)
    fw = fine_filters.reshape(3, 9, 128, 128)
    vmem = pl.BlockSpec(memory_space=pltpu.VMEM)
    anywhere = pl.BlockSpec(memory_space=pl.ANY)
    half = nz // 2
    dma = pltpu.SemaphoreType.DMA
    return pl.pallas_call(
        make_kernel(nz),
        out_shape=jax.ShapeDtypeStruct((8, 16, 8, 128), BF16),
        in_specs=[vmem, anywhere, vmem, anywhere, vmem, vmem],
        out_specs=vmem,
        scratch_shapes=[
            pltpu.VMEM((4, 64, 128), F32),
            pltpu.VMEM((16, 64, 512), BF16),
            pltpu.VMEM((9, 128, 512), BF16),
            pltpu.VMEM((9, 66, 16, 128), F32),
            pltpu.VMEM((2, 8, 16, 128), BF16),
            pltpu.VMEM((2, 8, 16, 128), BF16),
            pltpu.VMEM((16, 16, 128), F32),
            pltpu.VMEM((16, 16, 128), BF16),
            pltpu.VMEM((16, 16, 128), BF16),
            pltpu.VMEM((28 * outs, 256), BF16),
            pltpu.VMEM((28 * outs, 256), BF16),
            pltpu.VMEM((9, 256, 768), BF16),
            pltpu.VMEM((64, 512), BF16),
            pltpu.VMEM((64, 256), BF16),
            pltpu.VMEM((2, 32, 256), BF16),
            pltpu.VMEM((4, 16, 256), BF16),
            pltpu.VMEM((2, 16, 256), BF16),
            pltpu.VMEM((2, 32, 256), BF16),
            pltpu.VMEM((4, 16, 256), BF16),
            pltpu.VMEM((192, 768), BF16),
            pltpu.VMEM((9, 6, 4, 8, 256), F32),
            pltpu.VMEM((9, 384, 128), BF16),
            pltpu.VMEM((8, 4, 8, 128), F32),
            pltpu.VMEM((8, 4, 8, 128), F32),
            pltpu.VMEM((2, 32, 128), BF16),
            pltpu.VMEM((2, 64, 128), BF16),
            pltpu.VMEM((4, 16, 128), BF16),
            pltpu.VMEM((2, 32, 128), BF16),
            pltpu.VMEM((2, 64, 128), BF16),
            pltpu.VMEM((4, 16, 128), BF16),
            pltpu.VMEM((9, 10, 6, 8, 128), F32),
            pltpu.VMEM((1024, 128), F32),
            dma((6,)),
            dma((count_sends(nz),)),
            dma((2, 4)),
            dma((2, 4, 4)),
            dma((1,)),
            dma((2, half + 1)),
            dma((2 * half + 1,)),
            dma((2,)),
            dma((16,)),
            dma((8,)),
            dma((8,)),
        ],
        compiler_params=pltpu.CompilerParams(
            collective_id=0, has_side_effects=True, vmem_limit_bytes=50 * 1024 * 1024
        ),
    )(latent, cw, mw, fw, coarse_proj, mid_proj)


def solution(mesh):
    in_specs = (
        P(None, "grp", "tile", None),
        P(None, None, None, None, "grp"),
        P(None, None, None, None, "tile"),
        P(),
        P(),
        P(),
    )
    out_specs = P(None, "grp", "tile", None)
    return jax.shard_map(body, mesh=mesh, in_specs=in_specs, out_specs=out_specs, check_vma=False)
```

```python
import jax
import jax.numpy as jnp
from jax import lax
from jax.experimental import pallas as pl
from jax.experimental.pallas import tpu as pltpu
from jax.sharding import PartitionSpec as P

MESH = pl.DeviceIdType.MESH
F32 = jnp.float32
BF16 = jnp.bfloat16
NY = 4
NX = 4
NG = 16
NT_DIMS = (((1,), (1,)), ((), ()))
NN_DIMS = (((1,), (0,)), ((), ()))
SHIFTS = ((-1, 0, 0), (0, 0, 1))


def activate(values):
    scaled = values * lax.rsqrt(jnp.mean(values * values, axis=-1, keepdims=True) + 1e-06)
    return scaled / (1.0 + jnp.exp(-scaled))


def lane_group(rows):
    return lax.broadcasted_iota(jnp.int32, (rows, 128), 1) // 32


def pack_four(parts):
    group = lane_group(8)
    frame = lax.broadcasted_iota(jnp.int32, (8, 128), 0)
    one_back = (group == 1) & (frame >= 1)
    two_back = (group == 2) & (frame >= 2)
    total = None
    for k in range(4):
        mixed = jnp.where(
            group == 0, parts[k], jnp.where(group == 1, parts[(k + 1) % 4], parts[(k + 2) % 4])
        )
        moved = jnp.where(
            group == 0,
            mixed,
            jnp.where(
                one_back,
                pltpu.roll(mixed, 1, 0),
                jnp.where(two_back, pltpu.roll(mixed, 2, 0), 0.0),
            ),
        )
        turned = pltpu.roll(moved, 32 * k, 1) if k else moved
        total = turned if total is None else total + turned
    return total


def swap_groups(parts):
    rows = parts[0].shape[0]
    group = lane_group(rows)

    def pick(options):
        return jnp.where(
            group == 0,
            options[0],
            jnp.where(group == 1, options[1], jnp.where(group == 2, options[2], options[3])),
        )

    turned = []
    for k in range(4):
        mixed = pick([parts[(q + k) % 4] for q in range(4)])
        turned.append(pltpu.roll(mixed, 32 * k, 1) if k else mixed)
    return [pick([turned[(p - i) % 4] for p in range(4)]) for i in range(4)]


def frames_back(values, steps):
    frame = lax.broadcasted_iota(jnp.int32, values.shape, 1)
    return jnp.where(frame >= steps, pltpu.roll(values, steps, 1), 0.0)


def make_kernel(nz):
    nt = 2 * nz
    outs = 256 // nt
    half_ring = nz // 2

    def kernel(
        latent_hbm, cw_hbm, mw_hbm, fw_hbm, cproj_hbm, mproj_hbm, out,
        latent, mw, cproj, mproj, lat, gath, cw, prod, edge_out, edge_in, main, a2a_out, a2a_in,
        mine, theirs, wm, level, mrow, mcol, mcor, mrow_in, mcol_in, mcor_in,
        mx3, mprod, middle, fw, flow, fx, fprod, result,
        local_sem, send_sem, g1_sem, g2_sem, sib_sem, ring_sem, share_sem,
        edge_sem, a2a_sem, mh_sem,
    ):
        g = lax.axis_index("grp")
        t = lax.axis_index("tile")
        y, x = g // NX, g % NX
        z, core = t // 2, t % 2
        up_g, down_g = (g + NG - 1) % NG, (g + 1) % NG
        left_t, right_t = (t + nt - 1) % nt, (t + 1) % nt
        sib_t = z * 2 + 1 - core

        def gid(yy, xx):
            return ((yy + NY) % NY) * NX + (xx + NX) % NX

        def ring_t(dz):
            return ((z + dz + nz) % nz) * 2 + core

        sent = []

        def remote(src, dst, sem, dev):
            return pltpu.make_async_remote_copy(
                src_ref=src, dst_ref=dst, send_sem=send_sem.at[len(sent)], recv_sem=sem,
                device_id=dev, device_id_type=MESH,
            )

        def send(src, dst, sem, dev):
            copy = remote(src, dst, sem, dev)
            copy.start()
            sent.append(copy)

        def arrived(dst, sem):
            pltpu.make_async_remote_copy(
                src_ref=dst, dst_ref=dst, send_sem=send_sem.at[0], recv_sem=sem,
                device_id=(g, left_t), device_id_type=MESH,
            ).wait_recv()

        barrier = pltpu.get_barrier_semaphore()
        partners = [((g + d) % NG, t) for d in range(1, NG)]
        partners += [(g, left_t), (g, right_t), (g, ring_t(1)), (g, ring_t(-1))]
        partners += [(a, b) for a in (up_g, down_g) for b in (left_t, right_t)]
        for dev in partners:
            pl.semaphore_signal(barrier, inc=1, device_id=dev, device_id_type=MESH)

        early = [
            pltpu.make_async_copy(latent_hbm, latent, local_sem.at[6]),
            pltpu.make_async_copy(mw_hbm, mw, local_sem.at[7]),
        ]
        locals_ = [
            pltpu.make_async_copy(cproj_hbm, cproj, local_sem.at[8]),
            pltpu.make_async_copy(mproj_hbm, mproj, local_sem.at[9]),
        ]
        for a in range(3):
            locals_.append(
                pltpu.make_async_copy(
                    cw_hbm.at[a], cw.at[:, pl.ds(32 * (2 - a), 32), :], local_sem.at[a]
                )
            )
            locals_.append(
                pltpu.make_async_copy(
                    fw_hbm.at[a], fw.at[:, pl.ds(128 * a, 128), :], local_sem.at[3 + a]
                )
            )
        for copy in early + locals_:
            copy.start()
        for copy in early:
            copy.wait()

        for f in range(8):
            cells = latent[f].astype(F32).reshape(8, 512)
            for big in range(4):
                lat[big, pl.ds(8 * f, 8), :] = cells[:, 128 * big : 128 * big + 128]

        def lat_cell(big, cell):
            return lat[big, pl.ds(cell, 8, stride=8), :]

        own_lat = jnp.concatenate(
            [
                jnp.concatenate([lat_cell(big, cell) for big in range(4)], axis=1)
                for cell in range(8)
            ],
            axis=0,
        )
        gath[g] = activate(own_lat).astype(BF16)
        own_mw = jnp.concatenate(
            [mw[...].astype(F32), jnp.zeros((1, outs, 256), F32)], axis=0
        )
        mine[...] = own_mw.reshape(28 * outs, 256).astype(BF16)
        cw[:, pl.ds(96, 32), :] = jnp.zeros((9, 32, 512), BF16)
        prod[:, 0] = jnp.zeros((9, 16, 128), F32)
        prod[:, 65] = jnp.zeros((9, 16, 128), F32)

        pl.semaphore_wait(barrier, len(partners))

        def near(h, axis, d):
            along_x = (axis == 1) == (h == 0)
            return (gid(y, x + d), t) if along_x else (gid(y + d, x), t)

        def shard(h, d1, d2):
            return gid(y + d2, x + d1) if h == 0 else gid(y + d1, x + d2)

        def part(h, d1, d2, first, count):
            return gath.at[shard(h, d1, d2), pl.ds(32 * h + first, count), :]

        steps = (0, -1, 1, 2)
        ways = (1, -1, 2)

        def first(h):
            src = part(h, 0, 0, 0, 32)
            for n, way in enumerate(ways):
                send(src, src, g1_sem.at[h, n], near(h, 1, way))

        def second(h, k):
            src = part(h, steps[k], 0, 0, 32)
            for n, way in enumerate(ways):
                send(src, src, g2_sem.at[h, k, n], near(h, 2, way))

        send(mine, theirs, sib_sem.at[0], (g, sib_t))
        for h in range(2):
            first(h)
        for h in range(2):
            second(h, 0)

        arrived(theirs, sib_sem.at[0])
        own_f = mine[...].astype(F32).reshape(28, outs, 256)
        other_f = theirs[...].astype(F32).reshape(28, outs, 256)
        even = (jnp.zeros((1, 1, 256), jnp.int32) + core) == 0
        joined = jnp.concatenate(
            [jnp.where(even, own_f, other_f), jnp.where(even, other_f, own_f)], axis=1
        )
        rows_z = pl.multiple_of(2 * outs * z, 16)
        for a in range(3):
            for qh in range(2):
                wm[:, pl.ds(rows_z, 2 * outs), pl.ds(384 * qh + 128 * a, 128)] = joined[
                    9 * a : 9 * a + 9, :, 128 * qh : 128 * qh + 128
                ].astype(BF16)

        cuts = ((0, 5), (5, 4))

        def block(dz, core_at, cut=(0, 9)):
            row = pl.multiple_of(2 * outs * ((z + dz + nz) % nz), 16)
            lane = pl.multiple_of(384 * core_at, 128)
            return wm.at[pl.ds(*cut), pl.ds(row, 2 * outs), pl.ds(lane, 384)]

        sign = 1 - 2 * core

        def ring_send(k, n):
            if k < half_ring:
                src = block(1 - k, core, cuts[n])
                send(src, src, ring_sem.at[0, k, n], (g, ring_t(1)))
                src = block(k - 1, core, cuts[n])
                send(src, src, ring_sem.at[1, k, n], (g, ring_t(-1)))
            elif k == half_ring:
                src = block(-sign * (k - 1), core, cuts[n])
                send(src, src, ring_sem.at[0, k, n], (g, ring_t(sign)))

        def share(dz, slot):
            src = block(dz, core)
            send(src, src, share_sem.at[slot], (g, sib_t))

        def ring_event(k, n):
            arrived(block(-k, core, cuts[n]), ring_sem.at[0, k, n])
            if k < half_ring:
                arrived(block(k, core, cuts[n]), ring_sem.at[1, k, n])
            ring_send(k + 1, n)
            if n == 1:
                share(-k, 2 * k)
                if k < half_ring:
                    share(k, 2 * k + 1)

        events = [(k, n) for k in range(1, half_ring + 1) for n in range(2)]

        def poll(count):
            for _ in range(min(count, len(events))):
                ring_event(*events.pop(0))

        for n in range(2):
            ring_send(1, n)

        def coarse_chunk(d2):
            names = [(h, d1) for h in range(2) for d1 in steps]
            acts = jnp.concatenate([part(h, d1, d2, 0, 32)[...] for h, d1 in names], axis=0)
            for b in range(3):
                found = lax.dot_general(
                    acts, cw[pl.ds(3 * b, 3)].reshape(384, 512), NT_DIMS,
                    preferred_element_type=F32,
                )
                for n, (h, d1) in enumerate(names):
                    row = 4 * shard(h, d1, d2) + 2 * h + 1
                    for c in range(3):
                        prod[3 * b + c, pl.ds(row, 2)] = found[
                            32 * n : 32 * n + 32, 128 * c : 128 * c + 128
                        ].reshape(2, 16, 128)

        for k in (1, 2, 3):
            for h in range(2):
                arrived(part(h, steps[k], 0, 0, 32), g1_sem.at[h, k - 1])
                second(h, k)
        for copy in locals_:
            copy.wait()
        coarse_chunk(0)
        poll(2)
        for n, way in enumerate(ways):
            for k in range(4):
                for h in range(2):
                    arrived(part(h, steps[k], -way if n < 2 else 2, 0, 32), g2_sem.at[h, k, n])
            coarse_chunk(-way if n < 2 else 2)
            poll(1)
        poll(1)

        def taps(row, c, j):
            return sum(prod[3 * b + c, row + b, pl.ds(8 * j, 8), :] for b in range(3))

        def edges(rr, _):
            for e, (c, j) in enumerate(((2, 0), (0, 1))):
                both = [
                    pack_four([taps(8 * rr + 4 * s + i, c, j) for i in range(4)]) for s in range(2)
                ]
                edge_out[e, rr] = jnp.concatenate(both, axis=0).astype(BF16)
            return 0

        lax.fori_loop(0, 8, edges, 0)
        poll(1)
        send(edge_out.at[0], edge_in.at[1], edge_sem.at[1], (g, left_t))
        send(edge_out.at[1], edge_in.at[0], edge_sem.at[0], (g, right_t))

        def mains(r, _):
            for j in range(2):
                main[r, pl.ds(8 * j, 8), :] = pack_four(
                    [
                        taps(4 * r + i, 1, j) + taps(4 * r + i, 2 if j == 0 else 0, 1 - j)
                        for i in range(4)
                    ]
                )
            return 0

        lax.fori_loop(0, 16, mains, 0)
        poll(1)

        def inside(condition, like):
            return (jnp.zeros(like, jnp.int32) + condition.astype(jnp.int32)) > 0

        has_left, has_right = t > 0, t < nt - 1
        has_up, has_down = g > 0, g < NG - 1

        for j, has in ((0, has_left), (1, has_right)):
            arrived(edge_in.at[j], edge_sem.at[j])
            added = edge_in[j].astype(F32).reshape(16, 8, 128)
            added = jnp.where(inside(has, (16, 8, 128)), added, 0.0)
            main[:, pl.ds(8 * j, 8), :] = main[:, pl.ds(8 * j, 8), :] + added
        a2a_out[...] = main[...].astype(BF16)

        for d in range(1, NG):
            r = (g + d) % NG
            send(a2a_out.at[r], a2a_in.at[g], a2a_sem.at[d], (r, t))
        a2a_in[g] = a2a_out[g]
        poll(3)
        for d in range(1, NG):
            arrived(a2a_in.at[(g + NG - d) % NG], a2a_sem.at[d])

        for big in range(4):
            found = swap_groups([a2a_in[4 * big + p].astype(F32) for p in range(4)])
            for i in range(4):
                cells = jnp.concatenate(
                    [
                        lat_cell(big, 2 * i + j)
                        for j in range(2)
                    ],
                    axis=0,
                )
                level[pl.ds(16 * i, 16), pl.ds(128 * big, 128)] = (cells + found[i]).astype(BF16)
        reduced = jnp.dot(level[...], cproj[...], preferred_element_type=F32)
        reduced = reduced.astype(BF16).astype(F32)
        mrow[0] = reduced[0:16].astype(BF16)
        mrow[1] = reduced[48:64].astype(BF16)
        cells = reduced.reshape(8, 8, 256)
        for j in range(2):
            mcol[j] = jnp.concatenate(
                [reduced[16 * i + 8 * j : 16 * i + 8 * j + 8] for i in range(4)], axis=0
            ).astype(BF16)
            for i in range(2):
                corner = cells[6 * i + j]
                mcor[2 * i + j] = jnp.concatenate([corner, corner], axis=0).astype(BF16)

        def halo(row_first, row_last, col, cor, row_in, col_in, cor_in, sem):
            send(col.at[0], col_in.at[1], sem.at[3], (g, left_t))
            send(col.at[1], col_in.at[0], sem.at[2], (g, right_t))
            send(row_first, row_in.at[1], sem.at[1], (up_g, t))
            send(row_last, row_in.at[0], sem.at[0], (down_g, t))
            send(cor.at[0], cor_in.at[3], sem.at[7], (up_g, left_t))
            send(cor.at[1], cor_in.at[2], sem.at[6], (up_g, right_t))
            send(cor.at[2], cor_in.at[1], sem.at[5], (down_g, left_t))
            send(cor.at[3], cor_in.at[0], sem.at[4], (down_g, right_t))

        def halo_wait(row_in, col_in, cor_in, sem):
            for i in range(2):
                arrived(row_in.at[i], sem.at[i])
                arrived(col_in.at[i], sem.at[2 + i])
            for i in range(4):
                arrived(cor_in.at[i], sem.at[4 + i])

        halo(mrow.at[0], mrow.at[1], mcol, mcor, mrow_in, mcol_in, mcor_in, mh_sem)
        poll(2)
        halo_wait(mrow_in, mcol_in, mcor_in, mh_sem)

        def surround(center, row_in, col_in, cor_in, height, breadth):
            lanes = row_in.shape[-1]

            def keep(values, *conditions):
                for condition in conditions:
                    values = jnp.where(inside(condition, values.shape), values, 0.0)
                return values

            above = keep(row_in[0].astype(F32), has_up).reshape(breadth, 8, lanes)
            below = keep(row_in[1].astype(F32), has_down).reshape(breadth, 8, lanes)
            left = keep(col_in[0].astype(F32), has_left).reshape(height, 8, lanes)
            right = keep(col_in[1].astype(F32), has_right).reshape(height, 8, lanes)
            corner = [
                keep(cor_in[2 * i + j].astype(F32)[0:8], (has_up, has_down)[i], (has_left, has_right)[j])
                for i in range(2)
                for j in range(2)
            ]
            tiles = [corner[0]] + [above[j] for j in range(breadth)] + [corner[1]]
            for i in range(height):
                tiles += [left[i]] + [center(i, j) for j in range(breadth)] + [right[i]]
            tiles += [corner[2]] + [below[j] for j in range(breadth)] + [corner[3]]
            return jnp.concatenate([tile[None] for tile in tiles], axis=0)

        low = surround(lambda i, j: cells[2 * i + j], mrow_in, mcol_in, mcor_in, 4, 2)
        around = activate(low)
        for a in range(3):
            moved = frames_back(around, 2 - a) if a < 2 else around
            moved = moved.reshape(192, 256).astype(BF16)
            for qh in range(2):
                mx3[:, pl.ds(384 * qh + 128 * a, 128)] = moved[:, 128 * qh : 128 * qh + 128]
        poll(len(events))

        for k in range(1, half_ring):
            arrived(block(-k, 1 - core), share_sem.at[2 * k])
            arrived(block(k, 1 - core), share_sem.at[2 * k + 1])
        arrived(block(half_ring, 1 - core), share_sem.at[2 * half_ring])

        def mid_tap(bc, _):
            mprod[bc] = lax.dot_general(
                mx3[...], wm[bc], NT_DIMS, preferred_element_type=F32
            ).reshape(6, 4, 8, 256)
            return 0

        lax.fori_loop(0, 9, mid_tap, 0)

        low = low.reshape(6, 4, 8, 256)
        for pr in range(2):
            for pc in range(2):
                total = low[1 - pr : 6 - pr, 1 - pc : 4 - pc]
                for b in range(3):
                    row = SHIFTS[pr][b] + 1 - pr
                    for c in range(3):
                        col = SHIFTS[pc][c] + 1 - pc
                        total = total + mprod[3 * b + c, pl.ds(row, 5), pl.ds(col, 3)]
                middle[pl.ds(120 * (2 * pr + pc), 120), :] = total.reshape(120, 256)
        fine_low = jnp.dot(middle[...].astype(BF16), mproj[...], preferred_element_type=F32)
        fine_low = fine_low.astype(BF16).astype(F32)
        lively = activate(fine_low)
        for pr in range(2):
            for pc in range(2):
                for i in range(5):
                    for j in range(3):
                        row, col = 2 * i + 1 - pr, 2 * j + 1 - pc
                        at = 120 * (2 * pr + pc) + 8 * (3 * i + j)
                        tile = lively[at : at + 8]
                        for edge, has in (
                            (row == 0, has_up), (row == 9, has_down),
                            (col == 0, has_left), (col == 5, has_right),
                        ):
                            if edge:
                                tile = jnp.where(inside(has, (8, 128)), tile, 0.0)
                        fx[row, col] = tile
                        if 1 <= row <= 8 and 1 <= col <= 4:
                            flow[row - 1, col - 1] = fine_low[at : at + 8]

        around = fx[...].reshape(60, 8, 128)
        fine = jnp.concatenate(
            [
                (frames_back(around, 2 - a) if a < 2 else around).reshape(480, 128).astype(BF16)
                for a in range(3)
            ],
            axis=1,
        )
        for pair in range(5):
            names = [bc for bc in (2 * pair, 2 * pair + 1) if bc < 9]
            filters = jnp.concatenate([fw[bc] for bc in names], axis=1)
            found = lax.dot_general(fine, filters, NN_DIMS, preferred_element_type=F32)
            for n, bc in enumerate(names):
                fprod[bc] = found[:, 128 * n : 128 * n + 128].reshape(10, 6, 8, 128)

        for pr in range(2):
            for pc in range(2):
                for i in range(8):
                    for j in range(4):
                        total = flow[i, j]
                        for b in range(3):
                            for c in range(3):
                                total = total + fprod[
                                    3 * b + c, i + 1 + SHIFTS[pr][b], j + 1 + SHIFTS[pc][c]
                                ]
                        spot = 8 * (2 * i + pr) + 2 * j + pc
                        result[pl.ds(spot, 8, stride=128), :] = total
        out[...] = result[...].astype(BF16).reshape(8, 16, 8, 128)

        for copy in sent:
            copy.wait_send()

    return kernel


def count_sends(nz):
    ring = 2 * (nz // 2 - 1) + 1
    return 6 + 24 + 1 + 3 * ring + 2 + 15 + 8


def body(latent, coarse_filters, mid_filters, fine_filters, coarse_proj, mid_proj):
    nz = lax.axis_size("tile") // 2
    outs = mid_filters.shape[4]
    cw = jnp.transpose(coarse_filters, (0, 1, 2, 4, 3)).reshape(3, 9, 32, 512)
    mw = jnp.transpose(mid_filters, (0, 1, 2, 4, 3)).reshape(27, outs, 256)
    fw = fine_filters.reshape(3, 9, 128, 128)
    vmem = pl.BlockSpec(memory_space=pltpu.VMEM)
    half = nz // 2
    dma = pltpu.SemaphoreType.DMA
    return pl.pallas_call(
        make_kernel(nz),
        out_shape=jax.ShapeDtypeStruct((8, 16, 8, 128), BF16),
        in_specs=[pl.BlockSpec(memory_space=pl.ANY)] * 6,
        out_specs=vmem,
        scratch_shapes=[
            pltpu.VMEM((8, 4, 2, 512), BF16),
            pltpu.VMEM((27, outs, 256), BF16),
            pltpu.VMEM((512, 256), BF16),
            pltpu.VMEM((256, 128), BF16),
            pltpu.VMEM((4, 64, 128), F32),
            pltpu.VMEM((16, 64, 512), BF16),
            pltpu.VMEM((9, 128, 512), BF16),
            pltpu.VMEM((9, 66, 16, 128), F32),
            pltpu.VMEM((2, 8, 16, 128), BF16),
            pltpu.VMEM((2, 8, 16, 128), BF16),
            pltpu.VMEM((16, 16, 128), F32),
            pltpu.VMEM((16, 16, 128), BF16),
            pltpu.VMEM((16, 16, 128), BF16),
            pltpu.VMEM((28 * outs, 256), BF16),
            pltpu.VMEM((28 * outs, 256), BF16),
            pltpu.VMEM((9, 256, 768), BF16),
            pltpu.VMEM((64, 512), BF16),
            pltpu.VMEM((2, 16, 256), BF16),
            pltpu.VMEM((2, 32, 256), BF16),
            pltpu.VMEM((4, 16, 256), BF16),
            pltpu.VMEM((2, 16, 256), BF16),
            pltpu.VMEM((2, 32, 256), BF16),
            pltpu.VMEM((4, 16, 256), BF16),
            pltpu.VMEM((192, 768), BF16),
            pltpu.VMEM((9, 6, 4, 8, 256), F32),
            pltpu.VMEM((480, 256), F32),
            pltpu.VMEM((9, 384, 128), BF16),
            pltpu.VMEM((8, 4, 8, 128), F32),
            pltpu.VMEM((10, 6, 8, 128), F32),
            pltpu.VMEM((9, 10, 6, 8, 128), F32),
            pltpu.VMEM((1024, 128), F32),
            dma((10,)),
            dma((count_sends(nz),)),
            dma((2, 3)),
            dma((2, 4, 3)),
            dma((1,)),
            dma((2, half + 1, 2)),
            dma((2 * half + 1,)),
            dma((2,)),
            dma((16,)),
            dma((8,)),
        ],
        compiler_params=pltpu.CompilerParams(
            collective_id=0, has_side_effects=True, vmem_limit_bytes=60 * 1024 * 1024
        ),
    )(latent, cw, mw, fw, coarse_proj, mid_proj)


def solution(mesh):
    in_specs = (
        P(None, "grp", "tile", None),
        P(None, None, None, None, "grp"),
        P(None, None, None, None, "tile"),
        P(),
        P(),
        P(),
    )
    out_specs = P(None, "grp", "tile", None)
    return jax.shard_map(body, mesh=mesh, in_specs=in_specs, out_specs=out_specs, check_vma=False)
```

```python
import jax
import jax.numpy as jnp
from jax import lax
from jax.experimental import pallas as pl
from jax.experimental.pallas import tpu as pltpu
from jax.sharding import PartitionSpec as P

MESH = pl.DeviceIdType.MESH
F32 = jnp.float32
BF16 = jnp.bfloat16
NY = 4
NX = 4
NG = 16
NT_DIMS = (((1,), (1,)), ((), ()))
NN_DIMS = (((1,), (0,)), ((), ()))
POLLS = (3, 2, 3, 2, 2, 2, 4, 2, 4)
SHIFTS = ((-1, 0, 0), (0, 0, 1))


def activate(values):
    scaled = values * lax.rsqrt(jnp.mean(values * values, axis=-1, keepdims=True) + 1e-06)
    return scaled / (1.0 + jnp.exp(-scaled))


def lane_group(rows):
    return lax.broadcasted_iota(jnp.int32, (rows, 128), 1) // 32


def pack_four(parts):
    group = lane_group(8)
    frame = lax.broadcasted_iota(jnp.int32, (8, 128), 0)
    one_back = (group == 1) & (frame >= 1)
    two_back = (group == 2) & (frame >= 2)
    total = None
    for k in range(4):
        mixed = jnp.where(
            group == 0, parts[k], jnp.where(group == 1, parts[(k + 1) % 4], parts[(k + 2) % 4])
        )
        moved = jnp.where(
            group == 0,
            mixed,
            jnp.where(
                one_back,
                pltpu.roll(mixed, 1, 0),
                jnp.where(two_back, pltpu.roll(mixed, 2, 0), 0.0),
            ),
        )
        turned = pltpu.roll(moved, 32 * k, 1) if k else moved
        total = turned if total is None else total + turned
    return total


def swap_groups(parts):
    rows = parts[0].shape[0]
    group = lane_group(rows)

    def pick(options):
        return jnp.where(
            group == 0,
            options[0],
            jnp.where(group == 1, options[1], jnp.where(group == 2, options[2], options[3])),
        )

    turned = []
    for k in range(4):
        mixed = pick([parts[(q + k) % 4] for q in range(4)])
        turned.append(pltpu.roll(mixed, 32 * k, 1) if k else mixed)
    return [pick([turned[(p - i) % 4] for p in range(4)]) for i in range(4)]


def frames_back(values, steps):
    frame = lax.broadcasted_iota(jnp.int32, values.shape, 1)
    return jnp.where(frame >= steps, pltpu.roll(values, steps, 1), 0.0)


def make_kernel(nz):
    nt = 2 * nz
    outs = 256 // nt
    half_ring = nz // 2

    def kernel(
        latent_hbm, cw_hbm, mw_hbm, fw_hbm, cproj_hbm, mproj_hbm, out,
        latent, mw, cproj, mproj, lat, gath, cw, prod, edge_out, edge_in, main, a2a_out, a2a_in,
        mine, theirs, wm, level, mrow, mcol, mcor, mrow_in, mcol_in, mcor_in,
        mx3, mprod, middle, fw, flow, fx, fprod, result,
        local_sem, send_sem, g1_sem, g2_sem, sib_sem, ring_sem, share_sem,
        edge_sem, a2a_sem, mh_sem,
    ):
        g = lax.axis_index("grp")
        t = lax.axis_index("tile")
        y, x = g // NX, g % NX
        z, core = t // 2, t % 2
        up_g, down_g = (g + NG - 1) % NG, (g + 1) % NG
        left_t, right_t = (t + nt - 1) % nt, (t + 1) % nt
        sib_t = z * 2 + 1 - core

        def gid(yy, xx):
            return ((yy + NY) % NY) * NX + (xx + NX) % NX

        def ring_t(dz):
            return ((z + dz + nz) % nz) * 2 + core

        sent = []

        def remote(src, dst, sem, dev):
            return pltpu.make_async_remote_copy(
                src_ref=src, dst_ref=dst, send_sem=send_sem.at[len(sent)], recv_sem=sem,
                device_id=dev, device_id_type=MESH,
            )

        def send(src, dst, sem, dev):
            copy = remote(src, dst, sem, dev)
            copy.start()
            sent.append(copy)

        def arrived(dst, sem):
            pltpu.make_async_remote_copy(
                src_ref=dst, dst_ref=dst, send_sem=send_sem.at[0], recv_sem=sem,
                device_id=(g, left_t), device_id_type=MESH,
            ).wait_recv()

        barrier = pltpu.get_barrier_semaphore()
        partners = [((g + d) % NG, t) for d in range(1, NG)]
        partners += [(g, left_t), (g, right_t), (g, ring_t(1)), (g, ring_t(-1))]
        partners += [(a, b) for a in (up_g, down_g) for b in (left_t, right_t)]
        for dev in partners:
            pl.semaphore_signal(barrier, inc=1, device_id=dev, device_id_type=MESH)

        early = [
            pltpu.make_async_copy(latent_hbm, latent, local_sem.at[6]),
            pltpu.make_async_copy(mw_hbm, mw, local_sem.at[7]),
        ]
        locals_ = [
            pltpu.make_async_copy(cproj_hbm, cproj, local_sem.at[8]),
            pltpu.make_async_copy(mproj_hbm, mproj, local_sem.at[9]),
        ]
        for a in range(3):
            locals_.append(
                pltpu.make_async_copy(
                    cw_hbm.at[a], cw.at[:, pl.ds(32 * (2 - a), 32), :], local_sem.at[a]
                )
            )
            locals_.append(
                pltpu.make_async_copy(
                    fw_hbm.at[a], fw.at[:, pl.ds(128 * a, 128), :], local_sem.at[3 + a]
                )
            )
        for copy in early + locals_:
            copy.start()
        for copy in early:
            copy.wait()

        for f in range(8):
            cells = latent[f].astype(F32).reshape(8, 512)
            for big in range(4):
                lat[big, pl.ds(8 * f, 8), :] = cells[:, 128 * big : 128 * big + 128]

        def lat_cell(big, cell):
            return lat[big, pl.ds(cell, 8, stride=8), :]

        own_lat = jnp.concatenate(
            [
                jnp.concatenate([lat_cell(big, cell) for big in range(4)], axis=1)
                for cell in range(8)
            ],
            axis=0,
        )
        gath[g] = activate(own_lat).astype(BF16)
        own_mw = jnp.concatenate(
            [mw[...].astype(F32), jnp.zeros((1, outs, 256), F32)], axis=0
        )
        mine[...] = own_mw.reshape(28 * outs, 256).astype(BF16)
        cw[:, pl.ds(96, 32), :] = jnp.zeros((9, 32, 512), BF16)
        prod[:, 0] = jnp.zeros((9, 16, 128), F32)
        prod[:, 65] = jnp.zeros((9, 16, 128), F32)

        pl.semaphore_wait(barrier, len(partners))

        def near(h, axis, d):
            along_x = (axis == 1) == (h == 0)
            return (gid(y, x + d), t) if along_x else (gid(y + d, x), t)

        def shard(h, d1, d2):
            return gid(y + d2, x + d1) if h == 0 else gid(y + d1, x + d2)

        def part(h, d1, d2, first, count):
            return gath.at[shard(h, d1, d2), pl.ds(32 * h + first, count), :]

        steps = (0, -1, 1, 2)
        ways = (1, -1, 2)

        def first(h):
            src = part(h, 0, 0, 0, 32)
            for n, way in enumerate(ways):
                send(src, src, g1_sem.at[h, n], near(h, 1, way))

        def second(h, k):
            src = part(h, steps[k], 0, 0, 32)
            for n, way in enumerate(ways):
                send(src, src, g2_sem.at[h, k, n], near(h, 2, way))

        send(mine, theirs, sib_sem.at[0], (g, sib_t))
        for h in range(2):
            first(h)
        arrived(theirs, sib_sem.at[0])
        own_f = mine[...].astype(F32).reshape(28, outs, 256)
        other_f = theirs[...].astype(F32).reshape(28, outs, 256)
        even = (jnp.zeros((1, 1, 256), jnp.int32) + core) == 0
        joined = jnp.concatenate(
            [jnp.where(even, own_f, other_f), jnp.where(even, other_f, own_f)], axis=1
        )
        for a in range(3):
            for qh in range(2):
                wm[z, pl.ds(9 * qh, 9), :, pl.ds(128 * a, 128)] = joined[
                    9 * a : 9 * a + 9, :, 128 * qh : 128 * qh + 128
                ].astype(BF16)

        sign = 1 - 2 * core

        def block(dz, first, count):
            return wm.at[(z + dz + nz) % nz, pl.ds(first, count)]

        def ring_part(k, n, dz):
            if k < half_ring:
                return block(dz, 6 * n, 6)
            return block(dz, 9 * core + 3 * n, 3)

        def ring_send(k, n):
            if k <= half_ring:
                src = ring_part(k, n, -sign * (k - 1))
                send(src, src, ring_sem.at[k, n], (g, ring_t(sign)))

        def ring_event(k, n):
            arrived(ring_part(k, n, -sign * k), ring_sem.at[k, n])
            if k + 1 < half_ring:
                ring_send(k + 1, n)
            elif k + 1 == half_ring and n == 2:
                for m in range(3):
                    ring_send(k + 1, m)
            if n == 2:
                src = block(-sign * k, 0, 18) if k < half_ring else block(k, 9 * core, 9)
                send(src, src, share_sem.at[k], (g, sib_t))

        events = [(k, n) for k in range(1, half_ring + 1) for n in range(3)]

        def poll(count):
            for _ in range(min(count, len(events))):
                ring_event(*events.pop(0))

        for n in range(3):
            ring_send(1, n)
        for h in range(2):
            second(h, 0)

        def coarse_chunk(d2):
            names = [(h, d1) for h in range(2) for d1 in steps]
            acts = jnp.concatenate([part(h, d1, d2, 0, 32)[...] for h, d1 in names], axis=0)
            for b in range(3):
                found = lax.dot_general(
                    acts, cw[pl.ds(3 * b, 3)].reshape(384, 512), NT_DIMS,
                    preferred_element_type=F32,
                )
                for n, (h, d1) in enumerate(names):
                    row = 4 * shard(h, d1, d2) + 2 * h + 1
                    for c in range(3):
                        prod[3 * b + c, pl.ds(row, 2)] = found[
                            32 * n : 32 * n + 32, 128 * c : 128 * c + 128
                        ].reshape(2, 16, 128)

        for k in (1, 2, 3):
            for h in range(2):
                arrived(part(h, steps[k], 0, 0, 32), g1_sem.at[h, k - 1])
                second(h, k)
        for copy in locals_:
            copy.wait()
        coarse_chunk(0)
        poll(POLLS[0])
        for n, way in enumerate(ways):
            for k in range(4):
                for h in range(2):
                    arrived(part(h, steps[k], -way if n < 2 else 2, 0, 32), g2_sem.at[h, k, n])
            coarse_chunk(-way if n < 2 else 2)
            poll(POLLS[1 + n])

        def taps(row, c, j):
            return sum(prod[3 * b + c, row + b, pl.ds(8 * j, 8), :] for b in range(3))

        def edges(rr, _):
            for e, (c, j) in enumerate(((2, 0), (0, 1))):
                both = [
                    pack_four([taps(8 * rr + 4 * s + i, c, j) for i in range(4)]) for s in range(2)
                ]
                edge_out[e, rr] = jnp.concatenate(both, axis=0).astype(BF16)
            return 0

        lax.fori_loop(0, 8, edges, 0)
        send(edge_out.at[0], edge_in.at[1], edge_sem.at[1], (g, left_t))
        send(edge_out.at[1], edge_in.at[0], edge_sem.at[0], (g, right_t))
        poll(POLLS[4])

        def mains(r, _):
            for j in range(2):
                main[r, pl.ds(8 * j, 8), :] = pack_four(
                    [
                        taps(4 * r + i, 1, j) + taps(4 * r + i, 2 if j == 0 else 0, 1 - j)
                        for i in range(4)
                    ]
                )
            return 0

        lax.fori_loop(0, 16, mains, 0)
        poll(POLLS[5])

        def inside(condition, like):
            return (jnp.zeros(like, jnp.int32) + condition.astype(jnp.int32)) > 0

        has_left, has_right = t > 0, t < nt - 1
        has_up, has_down = g > 0, g < NG - 1

        for j, has in ((0, has_left), (1, has_right)):
            arrived(edge_in.at[j], edge_sem.at[j])
            added = edge_in[j].astype(F32).reshape(16, 8, 128)
            added = jnp.where(inside(has, (16, 8, 128)), added, 0.0)
            main[:, pl.ds(8 * j, 8), :] = main[:, pl.ds(8 * j, 8), :] + added
        a2a_out[...] = main[...].astype(BF16)

        for d in range(1, NG):
            r = (g + d) % NG
            send(a2a_out.at[r], a2a_in.at[g], a2a_sem.at[d], (r, t))
        a2a_in[g] = a2a_out[g]
        poll(POLLS[6])
        for d in range(1, NG):
            arrived(a2a_in.at[(g + NG - d) % NG], a2a_sem.at[d])
        poll(POLLS[7])

        for big in range(4):
            found = swap_groups([a2a_in[4 * big + p].astype(F32) for p in range(4)])
            for i in range(4):
                cells = jnp.concatenate(
                    [
                        lat_cell(big, 2 * i + j)
                        for j in range(2)
                    ],
                    axis=0,
                )
                level[pl.ds(16 * i, 16), pl.ds(128 * big, 128)] = (cells + found[i]).astype(BF16)
        reduced = jnp.dot(level[...], cproj[...], preferred_element_type=F32)
        reduced = reduced.astype(BF16).astype(F32)
        mrow[0] = reduced[0:16].astype(BF16)
        mrow[1] = reduced[48:64].astype(BF16)
        cells = reduced.reshape(8, 8, 256)
        for j in range(2):
            mcol[j] = jnp.concatenate(
                [reduced[16 * i + 8 * j : 16 * i + 8 * j + 8] for i in range(4)], axis=0
            ).astype(BF16)
            for i in range(2):
                corner = cells[6 * i + j]
                mcor[2 * i + j] = jnp.concatenate([corner, corner], axis=0).astype(BF16)

        def halo(row_first, row_last, col, cor, row_in, col_in, cor_in, sem):
            send(col.at[0], col_in.at[1], sem.at[3], (g, left_t))
            send(col.at[1], col_in.at[0], sem.at[2], (g, right_t))
            send(row_first, row_in.at[1], sem.at[1], (up_g, t))
            send(row_last, row_in.at[0], sem.at[0], (down_g, t))
            send(cor.at[0], cor_in.at[3], sem.at[7], (up_g, left_t))
            send(cor.at[1], cor_in.at[2], sem.at[6], (up_g, right_t))
            send(cor.at[2], cor_in.at[1], sem.at[5], (down_g, left_t))
            send(cor.at[3], cor_in.at[0], sem.at[4], (down_g, right_t))

        def halo_wait(row_in, col_in, cor_in, sem):
            for i in range(2):
                arrived(row_in.at[i], sem.at[i])
                arrived(col_in.at[i], sem.at[2 + i])
            for i in range(4):
                arrived(cor_in.at[i], sem.at[4 + i])

        halo(mrow.at[0], mrow.at[1], mcol, mcor, mrow_in, mcol_in, mcor_in, mh_sem)
        poll(POLLS[8])
        halo_wait(mrow_in, mcol_in, mcor_in, mh_sem)

        def surround(center, row_in, col_in, cor_in, height, breadth):
            lanes = row_in.shape[-1]

            def keep(values, *conditions):
                for condition in conditions:
                    values = jnp.where(inside(condition, values.shape), values, 0.0)
                return values

            above = keep(row_in[0].astype(F32), has_up).reshape(breadth, 8, lanes)
            below = keep(row_in[1].astype(F32), has_down).reshape(breadth, 8, lanes)
            left = keep(col_in[0].astype(F32), has_left).reshape(height, 8, lanes)
            right = keep(col_in[1].astype(F32), has_right).reshape(height, 8, lanes)
            corner = [
                keep(cor_in[2 * i + j].astype(F32)[0:8], (has_up, has_down)[i], (has_left, has_right)[j])
                for i in range(2)
                for j in range(2)
            ]
            tiles = [corner[0]] + [above[j] for j in range(breadth)] + [corner[1]]
            for i in range(height):
                tiles += [left[i]] + [center(i, j) for j in range(breadth)] + [right[i]]
            tiles += [corner[2]] + [below[j] for j in range(breadth)] + [corner[3]]
            return jnp.concatenate([tile[None] for tile in tiles], axis=0)

        low = surround(lambda i, j: cells[2 * i + j], mrow_in, mcol_in, mcor_in, 4, 2)
        around = activate(low)
        for a in range(3):
            moved = frames_back(around, 2 - a) if a < 2 else around
            moved = moved.reshape(192, 256).astype(BF16)
            for qh in range(2):
                mx3[:, pl.ds(384 * qh + 128 * a, 128)] = moved[:, 128 * qh : 128 * qh + 128]
        poll(len(events))

        for k in range(1, half_ring):
            arrived(block(sign * k, 0, 18), share_sem.at[k])
        arrived(block(half_ring, 9 * (1 - core), 9), share_sem.at[half_ring])

        def mid_tap(bc, _):
            filters = jnp.concatenate(
                [wm[:, bc + 9 * qh].reshape(256, 384) for qh in range(2)], axis=1
            )
            mprod[bc] = lax.dot_general(
                mx3[...], filters, NT_DIMS, preferred_element_type=F32
            ).reshape(6, 4, 8, 256)
            return 0

        lax.fori_loop(0, 9, mid_tap, 0)

        low = low.reshape(6, 4, 8, 256)
        for pr in range(2):
            for pc in range(2):
                total = low[1 - pr : 6 - pr, 1 - pc : 4 - pc]
                for b in range(3):
                    row = SHIFTS[pr][b] + 1 - pr
                    for c in range(3):
                        col = SHIFTS[pc][c] + 1 - pc
                        total = total + mprod[3 * b + c, pl.ds(row, 5), pl.ds(col, 3)]
                middle[pl.ds(120 * (2 * pr + pc), 120), :] = total.reshape(120, 256)
        fine_low = jnp.dot(middle[...].astype(BF16), mproj[...], preferred_element_type=F32)
        fine_low = fine_low.astype(BF16).astype(F32)
        lively = activate(fine_low)
        for pr in range(2):
            for pc in range(2):
                for i in range(5):
                    for j in range(3):
                        row, col = 2 * i + 1 - pr, 2 * j + 1 - pc
                        at = 120 * (2 * pr + pc) + 8 * (3 * i + j)
                        tile = lively[at : at + 8]
                        for edge, has in (
                            (row == 0, has_up), (row == 9, has_down),
                            (col == 0, has_left), (col == 5, has_right),
                        ):
                            if edge:
                                tile = jnp.where(inside(has, (8, 128)), tile, 0.0)
                        fx[row, col] = tile
                        if 1 <= row <= 8 and 1 <= col <= 4:
                            flow[row - 1, col - 1] = fine_low[at : at + 8]

        around = fx[...].reshape(60, 8, 128)
        fine = jnp.concatenate(
            [
                (frames_back(around, 2 - a) if a < 2 else around).reshape(480, 128).astype(BF16)
                for a in range(3)
            ],
            axis=1,
        )
        for pair in range(5):
            names = [bc for bc in (2 * pair, 2 * pair + 1) if bc < 9]
            filters = jnp.concatenate([fw[bc] for bc in names], axis=1)
            found = lax.dot_general(fine, filters, NN_DIMS, preferred_element_type=F32)
            for n, bc in enumerate(names):
                fprod[bc] = found[:, 128 * n : 128 * n + 128].reshape(10, 6, 8, 128)

        for pr in range(2):
            for pc in range(2):
                for i in range(8):
                    for j in range(4):
                        total = flow[i, j]
                        for b in range(3):
                            for c in range(3):
                                total = total + fprod[
                                    3 * b + c, i + 1 + SHIFTS[pr][b], j + 1 + SHIFTS[pc][c]
                                ]
                        spot = 8 * (2 * i + pr) + 2 * j + pc
                        result[pl.ds(spot, 8, stride=128), :] = total
        out[...] = result[...].astype(BF16).reshape(8, 16, 8, 128)

        for copy in sent:
            copy.wait_send()

    return kernel


def count_sends(nz):
    return 6 + 24 + 1 + 4 * (nz // 2) + 2 + 15 + 8


def body(latent, coarse_filters, mid_filters, fine_filters, coarse_proj, mid_proj):
    nz = lax.axis_size("tile") // 2
    outs = mid_filters.shape[4]
    cw = jnp.transpose(coarse_filters, (0, 1, 2, 4, 3)).reshape(3, 9, 32, 512)
    mw = jnp.transpose(mid_filters, (0, 1, 2, 4, 3)).reshape(27, outs, 256)
    fw = fine_filters.reshape(3, 9, 128, 128)
    vmem = pl.BlockSpec(memory_space=pltpu.VMEM)
    half = nz // 2
    dma = pltpu.SemaphoreType.DMA
    return pl.pallas_call(
        make_kernel(nz),
        out_shape=jax.ShapeDtypeStruct((8, 16, 8, 128), BF16),
        in_specs=[pl.BlockSpec(memory_space=pl.ANY)] * 6,
        out_specs=vmem,
        scratch_shapes=[
            pltpu.VMEM((8, 4, 2, 512), BF16),
            pltpu.VMEM((27, outs, 256), BF16),
            pltpu.VMEM((512, 256), BF16),
            pltpu.VMEM((256, 128), BF16),
            pltpu.VMEM((4, 64, 128), F32),
            pltpu.VMEM((16, 64, 512), BF16),
            pltpu.VMEM((9, 128, 512), BF16),
            pltpu.VMEM((9, 66, 16, 128), F32),
            pltpu.VMEM((2, 8, 16, 128), BF16),
            pltpu.VMEM((2, 8, 16, 128), BF16),
            pltpu.VMEM((16, 16, 128), F32),
            pltpu.VMEM((16, 16, 128), BF16),
            pltpu.VMEM((16, 16, 128), BF16),
            pltpu.VMEM((28 * outs, 256), BF16),
            pltpu.VMEM((28 * outs, 256), BF16),
            pltpu.VMEM((nz, 18, 2 * outs, 384), BF16),
            pltpu.VMEM((64, 512), BF16),
            pltpu.VMEM((2, 16, 256), BF16),
            pltpu.VMEM((2, 32, 256), BF16),
            pltpu.VMEM((4, 16, 256), BF16),
            pltpu.VMEM((2, 16, 256), BF16),
            pltpu.VMEM((2, 32, 256), BF16),
            pltpu.VMEM((4, 16, 256), BF16),
            pltpu.VMEM((192, 768), BF16),
            pltpu.VMEM((9, 6, 4, 8, 256), F32),
            pltpu.VMEM((480, 256), F32),
            pltpu.VMEM((9, 384, 128), BF16),
            pltpu.VMEM((8, 4, 8, 128), F32),
            pltpu.VMEM((10, 6, 8, 128), F32),
            pltpu.VMEM((9, 10, 6, 8, 128), F32),
            pltpu.VMEM((1024, 128), F32),
            dma((10,)),
            dma((count_sends(nz),)),
            dma((2, 3)),
            dma((2, 4, 3)),
            dma((1,)),
            dma((half + 1, 3)),
            dma((half + 1,)),
            dma((2,)),
            dma((16,)),
            dma((8,)),
        ],
        compiler_params=pltpu.CompilerParams(
            collective_id=0, has_side_effects=True, vmem_limit_bytes=60 * 1024 * 1024
        ),
    )(latent, cw, mw, fw, coarse_proj, mid_proj)


def solution(mesh):
    in_specs = (
        P(None, "grp", "tile", None),
        P(None, None, None, None, "grp"),
        P(None, None, None, None, "tile"),
        P(),
        P(),
        P(),
    )
    out_specs = P(None, "grp", "tile", None)
    return jax.shard_map(body, mesh=mesh, in_specs=in_specs, out_specs=out_specs, check_vma=False)
```

```python
import jax
import jax.numpy as jnp
from jax import lax
from jax.experimental import pallas as pl
from jax.experimental.pallas import tpu as pltpu
from jax.sharding import PartitionSpec as P

MESH = pl.DeviceIdType.MESH
F32 = jnp.float32
BF16 = jnp.bfloat16
NY = 4
NX = 4
NG = 16
NT_DIMS = (((1,), (1,)), ((), ()))
NN_DIMS = (((1,), (0,)), ((), ()))
POLLS = (3, 3, 3, 2, 2, 2, 3, 2, 4)
SHIFTS = ((-1, 0, 0), (0, 0, 1))


def activate(values):
    scaled = values * lax.rsqrt(jnp.mean(values * values, axis=-1, keepdims=True) + 1e-06)
    return scaled / (1.0 + jnp.exp(-scaled))


def lane_group(rows):
    return lax.broadcasted_iota(jnp.int32, (rows, 128), 1) // 32


def pack_four(parts):
    group = lane_group(8)
    frame = lax.broadcasted_iota(jnp.int32, (8, 128), 0)
    one_back = (group == 1) & (frame >= 1)
    two_back = (group == 2) & (frame >= 2)
    total = None
    for k in range(4):
        mixed = jnp.where(
            group == 0, parts[k], jnp.where(group == 1, parts[(k + 1) % 4], parts[(k + 2) % 4])
        )
        moved = jnp.where(
            group == 0,
            mixed,
            jnp.where(
                one_back,
                pltpu.roll(mixed, 1, 0),
                jnp.where(two_back, pltpu.roll(mixed, 2, 0), 0.0),
            ),
        )
        turned = pltpu.roll(moved, 32 * k, 1) if k else moved
        total = turned if total is None else total + turned
    return total


def swap_groups(parts):
    rows = parts[0].shape[0]
    group = lane_group(rows)

    def pick(options):
        return jnp.where(
            group == 0,
            options[0],
            jnp.where(group == 1, options[1], jnp.where(group == 2, options[2], options[3])),
        )

    turned = []
    for k in range(4):
        mixed = pick([parts[(q + k) % 4] for q in range(4)])
        turned.append(pltpu.roll(mixed, 32 * k, 1) if k else mixed)
    return [pick([turned[(p - i) % 4] for p in range(4)]) for i in range(4)]


def frames_back(values, steps):
    frame = lax.broadcasted_iota(jnp.int32, values.shape, 1)
    return jnp.where(frame >= steps, pltpu.roll(values, steps, 1), 0.0)


def make_kernel(nz):
    nt = 2 * nz
    outs = 256 // nt
    half_ring = nz // 2

    def kernel(
        latent_hbm, cw_hbm, mw_hbm, fw_hbm, cproj_hbm, mproj_hbm, out,
        latent, mw, cproj, mproj, lat, gath, cw, prod, edge_out, edge_in, main, a2a_out, a2a_in,
        mine, theirs, wm, level, mrow, mcol, mcor, mrow_in, mcol_in, mcor_in,
        mx3, mprod, middle, fw, flow, fx, fprod, result,
        local_sem, send_sem, g1_sem, g2_sem, sib_sem, ring_sem, share_sem,
        edge_sem, a2a_sem, mh_sem,
    ):
        g = lax.axis_index("grp")
        t = lax.axis_index("tile")
        y, x = g // NX, g % NX
        z, core = t // 2, t % 2
        up_g, down_g = (g + NG - 1) % NG, (g + 1) % NG
        left_t, right_t = (t + nt - 1) % nt, (t + 1) % nt
        sib_t = z * 2 + 1 - core

        def gid(yy, xx):
            return ((yy + NY) % NY) * NX + (xx + NX) % NX

        def ring_t(dz):
            return ((z + dz + nz) % nz) * 2 + core

        sent = []

        def remote(src, dst, sem, dev):
            return pltpu.make_async_remote_copy(
                src_ref=src, dst_ref=dst, send_sem=send_sem.at[len(sent)], recv_sem=sem,
                device_id=dev, device_id_type=MESH,
            )

        def send(src, dst, sem, dev):
            copy = remote(src, dst, sem, dev)
            copy.start()
            sent.append(copy)

        def arrived(dst, sem):
            pltpu.make_async_remote_copy(
                src_ref=dst, dst_ref=dst, send_sem=send_sem.at[0], recv_sem=sem,
                device_id=(g, left_t), device_id_type=MESH,
            ).wait_recv()

        early = [
            pltpu.make_async_copy(latent_hbm, latent, local_sem.at[6]),
            pltpu.make_async_copy(mw_hbm, mw, local_sem.at[7]),
        ]
        for copy in early:
            copy.start()

        barrier = pltpu.get_barrier_semaphore()
        partners = [((g + d) % NG, t) for d in range(1, NG)]
        partners += [(g, left_t), (g, right_t), (g, ring_t(1)), (g, ring_t(-1))]
        partners += [(a, b) for a in (up_g, down_g) for b in (left_t, right_t)]
        for dev in partners:
            pl.semaphore_signal(barrier, inc=1, device_id=dev, device_id_type=MESH)

        locals_ = [
            pltpu.make_async_copy(cproj_hbm, cproj, local_sem.at[8]),
            pltpu.make_async_copy(mproj_hbm, mproj, local_sem.at[9]),
        ]
        for a in range(3):
            locals_.append(
                pltpu.make_async_copy(
                    cw_hbm.at[a], cw.at[:, pl.ds(32 * (2 - a), 32), :], local_sem.at[a]
                )
            )
            locals_.append(
                pltpu.make_async_copy(
                    fw_hbm.at[a], fw.at[:, pl.ds(128 * a, 128), :], local_sem.at[3 + a]
                )
            )
        for copy in locals_:
            copy.start()
        for copy in early:
            copy.wait()

        for f in range(8):
            cells = latent[f].astype(F32).reshape(8, 512)
            for big in range(4):
                lat[big, pl.ds(8 * f, 8), :] = cells[:, 128 * big : 128 * big + 128]

        def lat_cell(big, cell):
            return lat[big, pl.ds(cell, 8, stride=8), :]

        own_lat = jnp.concatenate(
            [
                jnp.concatenate([lat_cell(big, cell) for big in range(4)], axis=1)
                for cell in range(8)
            ],
            axis=0,
        )
        gath[g] = activate(own_lat).astype(BF16)
        own_mw = jnp.concatenate(
            [mw[...].astype(F32), jnp.zeros((1, outs, 256), F32)], axis=0
        )
        mine[...] = own_mw.reshape(28 * outs, 256).astype(BF16)
        cw[:, pl.ds(96, 32), :] = jnp.zeros((9, 32, 512), BF16)
        prod[:, 0] = jnp.zeros((9, 16, 128), F32)
        prod[:, 65] = jnp.zeros((9, 16, 128), F32)

        pl.semaphore_wait(barrier, len(partners))

        def near(h, axis, d):
            along_x = (axis == 1) == (h == 0)
            return (gid(y, x + d), t) if along_x else (gid(y + d, x), t)

        def shard(h, d1, d2):
            return gid(y + d2, x + d1) if h == 0 else gid(y + d1, x + d2)

        def part(h, d1, d2, first, count):
            return gath.at[shard(h, d1, d2), pl.ds(32 * h + first, count), :]

        steps = (0, -1, 1, 2)
        ways = (1, -1, 2)

        def first(h):
            src = part(h, 0, 0, 0, 32)
            for n, way in enumerate(ways):
                send(src, src, g1_sem.at[h, n], near(h, 1, way))

        def second(h, k):
            src = part(h, steps[k], 0, 0, 32)
            for n, way in enumerate(ways):
                send(src, src, g2_sem.at[h, k, n], near(h, 2, way))

        send(mine, theirs, sib_sem.at[0], (g, sib_t))
        for h in range(2):
            first(h)
        arrived(theirs, sib_sem.at[0])
        own_f = mine[...].astype(F32).reshape(28, outs, 256)
        other_f = theirs[...].astype(F32).reshape(28, outs, 256)
        even = (jnp.zeros((1, 1, 256), jnp.int32) + core) == 0
        joined = jnp.concatenate(
            [jnp.where(even, own_f, other_f), jnp.where(even, other_f, own_f)], axis=1
        )
        for a in range(3):
            for qh in range(2):
                wm[z, pl.ds(9 * qh, 9), :, pl.ds(128 * a, 128)] = joined[
                    9 * a : 9 * a + 9, :, 128 * qh : 128 * qh + 128
                ].astype(BF16)

        sign = 1 - 2 * core

        def block(dz, first, count):
            return wm.at[(z + dz + nz) % nz, pl.ds(first, count)]

        def ring_part(k, n, dz):
            if k < half_ring:
                return block(dz, 6 * n, 6)
            return block(dz, 9 * core + 3 * n, 3)

        def ring_send(k, n):
            if k <= half_ring:
                src = ring_part(k, n, -sign * (k - 1))
                send(src, src, ring_sem.at[k, n], (g, ring_t(sign)))

        def ring_event(k, n):
            arrived(ring_part(k, n, -sign * k), ring_sem.at[k, n])
            if k + 1 < half_ring:
                ring_send(k + 1, n)
            elif k + 1 == half_ring and n == 2:
                for m in range(3):
                    ring_send(k + 1, m)
            if n == 2:
                src = block(-sign * k, 0, 18) if k < half_ring else block(k, 9 * core, 9)
                send(src, src, share_sem.at[k], (g, sib_t))

        events = [(k, n) for k in range(1, half_ring + 1) for n in range(3)]

        def poll(count):
            for _ in range(min(count, len(events))):
                ring_event(*events.pop(0))

        for n in range(3):
            ring_send(1, n)
        for h in range(2):
            second(h, 0)

        def coarse_chunk(d2):
            names = [(h, d1) for h in range(2) for d1 in steps]
            acts = jnp.concatenate([part(h, d1, d2, 0, 32)[...] for h, d1 in names], axis=0)
            for b in range(3):
                found = lax.dot_general(
                    acts, cw[pl.ds(3 * b, 3)].reshape(384, 512), NT_DIMS,
                    preferred_element_type=F32,
                )
                for n, (h, d1) in enumerate(names):
                    row = 4 * shard(h, d1, d2) + 2 * h + 1
                    for c in range(3):
                        prod[3 * b + c, pl.ds(row, 2)] = found[
                            32 * n : 32 * n + 32, 128 * c : 128 * c + 128
                        ].reshape(2, 16, 128)

        for k in (1, 2, 3):
            for h in range(2):
                arrived(part(h, steps[k], 0, 0, 32), g1_sem.at[h, k - 1])
                second(h, k)
        for copy in locals_:
            copy.wait()
        coarse_chunk(0)
        poll(POLLS[0])
        for n, way in enumerate(ways):
            for k in range(4):
                for h in range(2):
                    arrived(part(h, steps[k], -way if n < 2 else 2, 0, 32), g2_sem.at[h, k, n])
            coarse_chunk(-way if n < 2 else 2)
            poll(POLLS[1 + n])

        def taps(row, c, j):
            return sum(prod[3 * b + c, row + b, pl.ds(8 * j, 8), :] for b in range(3))

        def edges(rr, _):
            for e, (c, j) in enumerate(((2, 0), (0, 1))):
                both = [
                    pack_four([taps(8 * rr + 4 * s + i, c, j) for i in range(4)]) for s in range(2)
                ]
                edge_out[e, rr] = jnp.concatenate(both, axis=0).astype(BF16)
            return 0

        lax.fori_loop(0, 8, edges, 0, unroll=2)
        send(edge_out.at[0], edge_in.at[1], edge_sem.at[1], (g, left_t))
        send(edge_out.at[1], edge_in.at[0], edge_sem.at[0], (g, right_t))
        poll(POLLS[4])

        def mains(r, _):
            for j in range(2):
                main[r, pl.ds(8 * j, 8), :] = pack_four(
                    [
                        taps(4 * r + i, 1, j) + taps(4 * r + i, 2 if j == 0 else 0, 1 - j)
                        for i in range(4)
                    ]
                )
            return 0

        lax.fori_loop(0, 16, mains, 0, unroll=2)
        poll(POLLS[5])

        def inside(condition, like):
            return (jnp.zeros(like, jnp.int32) + condition.astype(jnp.int32)) > 0

        has_left, has_right = t > 0, t < nt - 1
        has_up, has_down = g > 0, g < NG - 1

        for j, has in ((0, has_left), (1, has_right)):
            arrived(edge_in.at[j], edge_sem.at[j])
            added = edge_in[j].astype(F32).reshape(16, 8, 128)
            added = jnp.where(inside(has, (16, 8, 128)), added, 0.0)
            main[:, pl.ds(8 * j, 8), :] = main[:, pl.ds(8 * j, 8), :] + added
        a2a_out[...] = main[...].astype(BF16)

        for d in range(1, NG):
            r = (g + d) % NG
            send(a2a_out.at[r], a2a_in.at[g], a2a_sem.at[d], (r, t))
        a2a_in[g] = a2a_out[g]
        poll(POLLS[6])
        for d in range(1, NG):
            arrived(a2a_in.at[(g + NG - d) % NG], a2a_sem.at[d])
        poll(POLLS[7])

        for big in range(4):
            found = swap_groups([a2a_in[4 * big + p].astype(F32) for p in range(4)])
            for i in range(4):
                cells = jnp.concatenate(
                    [
                        lat_cell(big, 2 * i + j)
                        for j in range(2)
                    ],
                    axis=0,
                )
                level[pl.ds(16 * i, 16), pl.ds(128 * big, 128)] = (cells + found[i]).astype(BF16)
        reduced = jnp.dot(level[...], cproj[...], preferred_element_type=F32)
        reduced = reduced.astype(BF16).astype(F32)
        mrow[0] = reduced[0:16].astype(BF16)
        mrow[1] = reduced[48:64].astype(BF16)
        cells = reduced.reshape(8, 8, 256)
        for j in range(2):
            mcol[j] = jnp.concatenate(
                [reduced[16 * i + 8 * j : 16 * i + 8 * j + 8] for i in range(4)], axis=0
            ).astype(BF16)
            for i in range(2):
                corner = cells[6 * i + j]
                mcor[2 * i + j] = jnp.concatenate([corner, corner], axis=0).astype(BF16)

        def halo(row_first, row_last, col, cor, row_in, col_in, cor_in, sem):
            send(col.at[0], col_in.at[1], sem.at[3], (g, left_t))
            send(col.at[1], col_in.at[0], sem.at[2], (g, right_t))
            send(row_first, row_in.at[1], sem.at[1], (up_g, t))
            send(row_last, row_in.at[0], sem.at[0], (down_g, t))
            send(cor.at[0], cor_in.at[3], sem.at[7], (up_g, left_t))
            send(cor.at[1], cor_in.at[2], sem.at[6], (up_g, right_t))
            send(cor.at[2], cor_in.at[1], sem.at[5], (down_g, left_t))
            send(cor.at[3], cor_in.at[0], sem.at[4], (down_g, right_t))

        def halo_wait(row_in, col_in, cor_in, sem):
            for i in range(2):
                arrived(row_in.at[i], sem.at[i])
                arrived(col_in.at[i], sem.at[2 + i])
            for i in range(4):
                arrived(cor_in.at[i], sem.at[4 + i])

        halo(mrow.at[0], mrow.at[1], mcol, mcor, mrow_in, mcol_in, mcor_in, mh_sem)
        poll(POLLS[8])
        halo_wait(mrow_in, mcol_in, mcor_in, mh_sem)

        def surround(center, row_in, col_in, cor_in, height, breadth):
            lanes = row_in.shape[-1]

            def keep(values, *conditions):
                for condition in conditions:
                    values = jnp.where(inside(condition, values.shape), values, 0.0)
                return values

            above = keep(row_in[0].astype(F32), has_up).reshape(breadth, 8, lanes)
            below = keep(row_in[1].astype(F32), has_down).reshape(breadth, 8, lanes)
            left = keep(col_in[0].astype(F32), has_left).reshape(height, 8, lanes)
            right = keep(col_in[1].astype(F32), has_right).reshape(height, 8, lanes)
            corner = [
                keep(cor_in[2 * i + j].astype(F32)[0:8], (has_up, has_down)[i], (has_left, has_right)[j])
                for i in range(2)
                for j in range(2)
            ]
            tiles = [corner[0]] + [above[j] for j in range(breadth)] + [corner[1]]
            for i in range(height):
                tiles += [left[i]] + [center(i, j) for j in range(breadth)] + [right[i]]
            tiles += [corner[2]] + [below[j] for j in range(breadth)] + [corner[3]]
            return jnp.concatenate([tile[None] for tile in tiles], axis=0)

        low = surround(lambda i, j: cells[2 * i + j], mrow_in, mcol_in, mcor_in, 4, 2)
        around = activate(low)
        for a in range(3):
            moved = frames_back(around, 2 - a) if a < 2 else around
            moved = moved.reshape(192, 256).astype(BF16)
            for qh in range(2):
                mx3[:, pl.ds(384 * qh + 128 * a, 128)] = moved[:, 128 * qh : 128 * qh + 128]
        poll(len(events))

        for k in range(1, half_ring):
            arrived(block(sign * k, 0, 18), share_sem.at[k])
        arrived(block(half_ring, 9 * (1 - core), 9), share_sem.at[half_ring])

        def mid_tap(bc, _):
            filters = jnp.concatenate(
                [wm[:, bc + 9 * qh].reshape(256, 384) for qh in range(2)], axis=1
            )
            mprod[bc] = lax.dot_general(
                mx3[...], filters, NT_DIMS, preferred_element_type=F32
            ).reshape(6, 4, 8, 256)
            return 0

        lax.fori_loop(0, 9, mid_tap, 0, unroll=9)

        low = low.reshape(6, 4, 8, 256)
        for pr in range(2):
            for pc in range(2):
                total = low[1 - pr : 6 - pr, 1 - pc : 4 - pc]
                for b in range(3):
                    row = SHIFTS[pr][b] + 1 - pr
                    for c in range(3):
                        col = SHIFTS[pc][c] + 1 - pc
                        total = total + mprod[3 * b + c, pl.ds(row, 5), pl.ds(col, 3)]
                middle[pl.ds(120 * (2 * pr + pc), 120), :] = total.reshape(120, 256)
        fine_low = jnp.dot(middle[...].astype(BF16), mproj[...], preferred_element_type=F32)
        fine_low = fine_low.astype(BF16).astype(F32)
        lively = activate(fine_low)
        for pr in range(2):
            for pc in range(2):
                for i in range(5):
                    for j in range(3):
                        row, col = 2 * i + 1 - pr, 2 * j + 1 - pc
                        at = 120 * (2 * pr + pc) + 8 * (3 * i + j)
                        tile = lively[at : at + 8]
                        for edge, has in (
                            (row == 0, has_up), (row == 9, has_down),
                            (col == 0, has_left), (col == 5, has_right),
                        ):
                            if edge:
                                tile = jnp.where(inside(has, (8, 128)), tile, 0.0)
                        fx[row, col] = tile
                        if 1 <= row <= 8 and 1 <= col <= 4:
                            flow[row - 1, col - 1] = fine_low[at : at + 8]

        around = fx[...].reshape(60, 8, 128)
        fine = jnp.concatenate(
            [
                (frames_back(around, 2 - a) if a < 2 else around).reshape(480, 128).astype(BF16)
                for a in range(3)
            ],
            axis=1,
        )
        for pair in range(5):
            names = [bc for bc in (2 * pair, 2 * pair + 1) if bc < 9]
            filters = jnp.concatenate([fw[bc] for bc in names], axis=1)
            found = lax.dot_general(fine, filters, NN_DIMS, preferred_element_type=F32)
            for n, bc in enumerate(names):
                fprod[bc] = found[:, 128 * n : 128 * n + 128].reshape(10, 6, 8, 128)

        for pr in range(2):
            for pc in range(2):
                for i in range(8):
                    for j in range(4):
                        total = flow[i, j]
                        for b in range(3):
                            for c in range(3):
                                total = total + fprod[
                                    3 * b + c, i + 1 + SHIFTS[pr][b], j + 1 + SHIFTS[pc][c]
                                ]
                        spot = 8 * (2 * i + pr) + 2 * j + pc
                        result[pl.ds(spot, 8, stride=128), :] = total
        out[...] = result[...].astype(BF16).reshape(8, 16, 8, 128)

        for copy in sent:
            copy.wait_send()

    return kernel


def count_sends(nz):
    return 6 + 24 + 1 + 4 * (nz // 2) + 2 + 15 + 8


def body(latent, coarse_filters, mid_filters, fine_filters, coarse_proj, mid_proj):
    nz = lax.axis_size("tile") // 2
    outs = mid_filters.shape[4]
    cw = jnp.transpose(coarse_filters, (0, 1, 2, 4, 3)).reshape(3, 9, 32, 512)
    mw = jnp.transpose(mid_filters, (0, 1, 2, 4, 3)).reshape(27, outs, 256)
    fw = fine_filters.reshape(3, 9, 128, 128)
    vmem = pl.BlockSpec(memory_space=pltpu.VMEM)
    half = nz // 2
    dma = pltpu.SemaphoreType.DMA
    return pl.pallas_call(
        make_kernel(nz),
        out_shape=jax.ShapeDtypeStruct((8, 16, 8, 128), BF16),
        in_specs=[pl.BlockSpec(memory_space=pl.ANY)] * 6,
        out_specs=vmem,
        scratch_shapes=[
            pltpu.VMEM((8, 4, 2, 512), BF16),
            pltpu.VMEM((27, outs, 256), BF16),
            pltpu.VMEM((512, 256), BF16),
            pltpu.VMEM((256, 128), BF16),
            pltpu.VMEM((4, 64, 128), F32),
            pltpu.VMEM((16, 64, 512), BF16),
            pltpu.VMEM((9, 128, 512), BF16),
            pltpu.VMEM((9, 66, 16, 128), F32),
            pltpu.VMEM((2, 8, 16, 128), BF16),
            pltpu.VMEM((2, 8, 16, 128), BF16),
            pltpu.VMEM((16, 16, 128), F32),
            pltpu.VMEM((16, 16, 128), BF16),
            pltpu.VMEM((16, 16, 128), BF16),
            pltpu.VMEM((28 * outs, 256), BF16),
            pltpu.VMEM((28 * outs, 256), BF16),
            pltpu.VMEM((nz, 18, 2 * outs, 384), BF16),
            pltpu.VMEM((64, 512), BF16),
            pltpu.VMEM((2, 16, 256), BF16),
            pltpu.VMEM((2, 32, 256), BF16),
            pltpu.VMEM((4, 16, 256), BF16),
            pltpu.VMEM((2, 16, 256), BF16),
            pltpu.VMEM((2, 32, 256), BF16),
            pltpu.VMEM((4, 16, 256), BF16),
            pltpu.VMEM((192, 768), BF16),
            pltpu.VMEM((9, 6, 4, 8, 256), F32),
            pltpu.VMEM((480, 256), F32),
            pltpu.VMEM((9, 384, 128), BF16),
            pltpu.VMEM((8, 4, 8, 128), F32),
            pltpu.VMEM((10, 6, 8, 128), F32),
            pltpu.VMEM((9, 10, 6, 8, 128), F32),
            pltpu.VMEM((1024, 128), F32),
            dma((10,)),
            dma((count_sends(nz),)),
            dma((2, 3)),
            dma((2, 4, 3)),
            dma((1,)),
            dma((half + 1, 3)),
            dma((half + 1,)),
            dma((2,)),
            dma((16,)),
            dma((8,)),
        ],
        compiler_params=pltpu.CompilerParams(
            collective_id=0, has_side_effects=True, vmem_limit_bytes=60 * 1024 * 1024
        ),
    )(latent, cw, mw, fw, coarse_proj, mid_proj)


def solution(mesh):
    in_specs = (
        P(None, "grp", "tile", None),
        P(None, None, None, None, "grp"),
        P(None, None, None, None, "tile"),
        P(),
        P(),
        P(),
    )
    out_specs = P(None, "grp", "tile", None)
    return jax.shard_map(body, mesh=mesh, in_specs=in_specs, out_specs=out_specs, check_vma=False)
```

```python
import jax
import jax.numpy as jnp
from jax import lax
from jax.experimental import pallas as pl
from jax.experimental.pallas import tpu as pltpu
from jax.sharding import PartitionSpec as P

MESH = pl.DeviceIdType.MESH
F32 = jnp.float32
BF16 = jnp.bfloat16
NY = 4
NX = 4
NG = 16
NT_DIMS = (((1,), (1,)), ((), ()))
NN_DIMS = (((1,), (0,)), ((), ()))
POLLS = (4, 3, 3, 3, 2, 2, 3, 1, 3)
SHIFTS = ((-1, 0, 0), (0, 0, 1))


def activate(values):
    scaled = values * lax.rsqrt(jnp.mean(values * values, axis=-1, keepdims=True) + 1e-06)
    return scaled / (1.0 + jnp.exp(-scaled))


def lane_group(rows):
    return lax.broadcasted_iota(jnp.int32, (rows, 128), 1) // 32


def pack_four(parts):
    group = lane_group(8)
    frame = lax.broadcasted_iota(jnp.int32, (8, 128), 0)
    one_back = (group == 1) & (frame >= 1)
    two_back = (group == 2) & (frame >= 2)
    total = None
    for k in range(4):
        mixed = jnp.where(
            group == 0, parts[k], jnp.where(group == 1, parts[(k + 1) % 4], parts[(k + 2) % 4])
        )
        moved = jnp.where(
            group == 0,
            mixed,
            jnp.where(
                one_back,
                pltpu.roll(mixed, 1, 0),
                jnp.where(two_back, pltpu.roll(mixed, 2, 0), 0.0),
            ),
        )
        turned = pltpu.roll(moved, 32 * k, 1) if k else moved
        total = turned if total is None else total + turned
    return total


def swap_groups(parts):
    rows = parts[0].shape[0]
    group = lane_group(rows)

    def pick(options):
        return jnp.where(
            group == 0,
            options[0],
            jnp.where(group == 1, options[1], jnp.where(group == 2, options[2], options[3])),
        )

    turned = []
    for k in range(4):
        mixed = pick([parts[(q + k) % 4] for q in range(4)])
        turned.append(pltpu.roll(mixed, 32 * k, 1) if k else mixed)
    return [pick([turned[(p - i) % 4] for p in range(4)]) for i in range(4)]


def frames_back(values, steps):
    frame = lax.broadcasted_iota(jnp.int32, values.shape, 1)
    return jnp.where(frame >= steps, pltpu.roll(values, steps, 1), 0.0)


def make_kernel(nz):
    nt = 2 * nz
    outs = 256 // nt
    half_ring = nz // 2

    def kernel(
        latent_hbm, cw_hbm, mw_hbm, fw_hbm, cproj_hbm, mproj_hbm, out,
        latent, mw, cproj, mproj, lat, gath, cw, prod, edge_out, edge_in, main, a2a_out, a2a_in,
        mine, theirs, wm, level, mrow, mcol, mcor, mrow_in, mcol_in, mcor_in,
        mx3, mprod, middle, fw, flow, fx, fprod, result,
        local_sem, send_sem, g1_sem, g2_sem, sib_sem, ring_sem, share_sem,
        edge_sem, a2a_sem, mh_sem,
    ):
        g = lax.axis_index("grp")
        t = lax.axis_index("tile")
        y, x = g // NX, g % NX
        z, core = t // 2, t % 2
        up_g, down_g = (g + NG - 1) % NG, (g + 1) % NG
        left_t, right_t = (t + nt - 1) % nt, (t + 1) % nt
        sib_t = z * 2 + 1 - core

        def gid(yy, xx):
            return ((yy + NY) % NY) * NX + (xx + NX) % NX

        def ring_t(dz):
            return ((z + dz + nz) % nz) * 2 + core

        sent = []

        def remote(src, dst, sem, dev):
            return pltpu.make_async_remote_copy(
                src_ref=src, dst_ref=dst, send_sem=send_sem.at[len(sent)], recv_sem=sem,
                device_id=dev, device_id_type=MESH,
            )

        def send(src, dst, sem, dev):
            copy = remote(src, dst, sem, dev)
            copy.start()
            sent.append(copy)

        def arrived(dst, sem):
            pltpu.make_async_remote_copy(
                src_ref=dst, dst_ref=dst, send_sem=send_sem.at[0], recv_sem=sem,
                device_id=(g, left_t), device_id_type=MESH,
            ).wait_recv()

        early = [
            pltpu.make_async_copy(latent_hbm, latent, local_sem.at[6]),
            pltpu.make_async_copy(mw_hbm, mw, local_sem.at[7]),
        ]
        for copy in early:
            copy.start()

        barrier = pltpu.get_barrier_semaphore()
        partners = [((g + d) % NG, t) for d in range(1, NG)]
        partners += [(g, left_t), (g, right_t), (g, ring_t(1)), (g, ring_t(-1))]
        partners += [(a, b) for a in (up_g, down_g) for b in (left_t, right_t)]
        for dev in partners:
            pl.semaphore_signal(barrier, inc=1, device_id=dev, device_id_type=MESH)

        locals_ = [
            pltpu.make_async_copy(cproj_hbm, cproj, local_sem.at[8]),
            pltpu.make_async_copy(mproj_hbm, mproj, local_sem.at[9]),
        ]
        for a in range(3):
            locals_.append(
                pltpu.make_async_copy(
                    cw_hbm.at[a], cw.at[:, pl.ds(32 * (2 - a), 32), :], local_sem.at[a]
                )
            )
            locals_.append(
                pltpu.make_async_copy(
                    fw_hbm.at[a], fw.at[:, pl.ds(128 * a, 128), :], local_sem.at[3 + a]
                )
            )
        for copy in locals_:
            copy.start()
        for copy in early:
            copy.wait()

        for f in range(8):
            cells = latent[f].astype(F32).reshape(8, 512)
            for big in range(4):
                lat[big, pl.ds(8 * f, 8), :] = cells[:, 128 * big : 128 * big + 128]

        def lat_cell(big, cell):
            return lat[big, pl.ds(cell, 8, stride=8), :]

        own_lat = jnp.concatenate(
            [
                jnp.concatenate([lat_cell(big, cell) for big in range(4)], axis=1)
                for cell in range(8)
            ],
            axis=0,
        )
        gath[g] = activate(own_lat).astype(BF16)
        own_mw = jnp.concatenate(
            [mw[...].astype(F32), jnp.zeros((1, outs, 256), F32)], axis=0
        )
        mine[...] = own_mw.reshape(28 * outs, 256).astype(BF16)
        cw[:, pl.ds(96, 32), :] = jnp.zeros((9, 32, 512), BF16)
        prod[:, 0] = jnp.zeros((9, 16, 128), F32)
        prod[:, 65] = jnp.zeros((9, 16, 128), F32)

        pl.semaphore_wait(barrier, len(partners))

        def near(h, axis, d):
            along_x = (axis == 1) == (h == 0)
            return (gid(y, x + d), t) if along_x else (gid(y + d, x), t)

        def shard(h, d1, d2):
            return gid(y + d2, x + d1) if h == 0 else gid(y + d1, x + d2)

        def part(h, d1, d2, first, count):
            return gath.at[shard(h, d1, d2), pl.ds(32 * h + first, count), :]

        steps = (0, -1, 1, 2)
        ways = (1, -1, 2)

        def first(h):
            src = part(h, 0, 0, 0, 32)
            for n, way in enumerate(ways):
                send(src, src, g1_sem.at[h, n], near(h, 1, way))

        def second(h, k):
            src = part(h, steps[k], 0, 0, 32)
            for n, way in enumerate(ways):
                send(src, src, g2_sem.at[h, k, n], near(h, 2, way))

        send(mine, theirs, sib_sem.at[0], (g, sib_t))
        for h in range(2):
            first(h)
        arrived(theirs, sib_sem.at[0])
        own_f = mine[...].astype(F32).reshape(28, outs, 256)
        other_f = theirs[...].astype(F32).reshape(28, outs, 256)
        even = (jnp.zeros((1, 1, 256), jnp.int32) + core) == 0
        joined = jnp.concatenate(
            [jnp.where(even, own_f, other_f), jnp.where(even, other_f, own_f)], axis=1
        )
        for a in range(3):
            for qh in range(2):
                wm[z, pl.ds(9 * qh, 9), :, pl.ds(128 * a, 128)] = joined[
                    9 * a : 9 * a + 9, :, 128 * qh : 128 * qh + 128
                ].astype(BF16)

        sign = 1 - 2 * core

        def block(dz, first, count):
            return wm.at[(z + dz + nz) % nz, pl.ds(first, count)]

        def ring_part(k, n, dz):
            if k < half_ring:
                return block(dz, 6 * n, 6)
            return block(dz, 9 * core + 3 * n, 3)

        def ring_send(k, n):
            if k <= half_ring:
                src = ring_part(k, n, -sign * (k - 1))
                send(src, src, ring_sem.at[k, n], (g, ring_t(sign)))

        def ring_event(k, n):
            arrived(ring_part(k, n, -sign * k), ring_sem.at[k, n])
            if k + 1 < half_ring:
                ring_send(k + 1, n)
            elif k + 1 == half_ring and n == 2:
                for m in range(3):
                    ring_send(k + 1, m)
            if n == 2:
                src = block(-sign * k, 0, 18) if k < half_ring else block(k, 9 * core, 9)
                send(src, src, share_sem.at[k], (g, sib_t))

        events = [(k, n) for k in range(1, half_ring + 1) for n in range(3)]

        def poll(count):
            for _ in range(min(count, len(events))):
                ring_event(*events.pop(0))

        for n in range(3):
            ring_send(1, n)
        for h in range(2):
            second(h, 0)

        def coarse_chunk(d2):
            names = [(h, d1) for h in range(2) for d1 in steps]
            acts = jnp.concatenate([part(h, d1, d2, 0, 32)[...] for h, d1 in names], axis=0)
            for b in range(3):
                found = lax.dot_general(
                    acts, cw[pl.ds(3 * b, 3)].reshape(384, 512), NT_DIMS,
                    preferred_element_type=F32,
                )
                for n, (h, d1) in enumerate(names):
                    row = 4 * shard(h, d1, d2) + 2 * h + 1
                    for c in range(3):
                        prod[3 * b + c, pl.ds(row, 2)] = found[
                            32 * n : 32 * n + 32, 128 * c : 128 * c + 128
                        ].reshape(2, 16, 128)

        for k in (1, 2, 3):
            for h in range(2):
                arrived(part(h, steps[k], 0, 0, 32), g1_sem.at[h, k - 1])
                second(h, k)
        for copy in locals_:
            copy.wait()
        coarse_chunk(0)
        poll(POLLS[0])
        for n, way in enumerate(ways):
            for k in range(4):
                for h in range(2):
                    arrived(part(h, steps[k], -way if n < 2 else 2, 0, 32), g2_sem.at[h, k, n])
            coarse_chunk(-way if n < 2 else 2)
            poll(POLLS[1 + n])

        def taps(row, c, j):
            return sum(prod[3 * b + c, row + b, pl.ds(8 * j, 8), :] for b in range(3))

        def edges(rr, _):
            for e, (c, j) in enumerate(((2, 0), (0, 1))):
                both = [
                    pack_four([taps(8 * rr + 4 * s + i, c, j) for i in range(4)]) for s in range(2)
                ]
                edge_out[e, rr] = jnp.concatenate(both, axis=0).astype(BF16)
            return 0

        lax.fori_loop(0, 8, edges, 0, unroll=4)
        send(edge_out.at[0], edge_in.at[1], edge_sem.at[1], (g, left_t))
        send(edge_out.at[1], edge_in.at[0], edge_sem.at[0], (g, right_t))
        poll(POLLS[4])

        def mains(r, _):
            for j in range(2):
                main[r, pl.ds(8 * j, 8), :] = pack_four(
                    [
                        taps(4 * r + i, 1, j) + taps(4 * r + i, 2 if j == 0 else 0, 1 - j)
                        for i in range(4)
                    ]
                )
            return 0

        lax.fori_loop(0, 16, mains, 0, unroll=8)
        poll(POLLS[5])

        def inside(condition, like):
            return (jnp.zeros(like, jnp.int32) + condition.astype(jnp.int32)) > 0

        has_left, has_right = t > 0, t < nt - 1
        has_up, has_down = g > 0, g < NG - 1

        for j, has in ((0, has_left), (1, has_right)):
            arrived(edge_in.at[j], edge_sem.at[j])
            added = edge_in[j].astype(F32).reshape(16, 8, 128)
            added = jnp.where(inside(has, (16, 8, 128)), added, 0.0)
            main[:, pl.ds(8 * j, 8), :] = main[:, pl.ds(8 * j, 8), :] + added
        a2a_out[...] = main[...].astype(BF16)

        for d in range(1, NG):
            r = (g + d) % NG
            send(a2a_out.at[r], a2a_in.at[g], a2a_sem.at[d], (r, t))
        a2a_in[g] = a2a_out[g]
        poll(POLLS[6])
        for d in range(1, NG):
            arrived(a2a_in.at[(g + NG - d) % NG], a2a_sem.at[d])
        poll(POLLS[7])

        for big in range(4):
            found = swap_groups([a2a_in[4 * big + p].astype(F32) for p in range(4)])
            for i in range(4):
                cells = jnp.concatenate(
                    [
                        lat_cell(big, 2 * i + j)
                        for j in range(2)
                    ],
                    axis=0,
                )
                level[pl.ds(16 * i, 16), pl.ds(128 * big, 128)] = (cells + found[i]).astype(BF16)
        reduced = jnp.dot(level[...], cproj[...], preferred_element_type=F32)
        reduced = reduced.astype(BF16).astype(F32)
        mrow[0] = reduced[0:16].astype(BF16)
        mrow[1] = reduced[48:64].astype(BF16)
        cells = reduced.reshape(8, 8, 256)
        for j in range(2):
            mcol[j] = jnp.concatenate(
                [reduced[16 * i + 8 * j : 16 * i + 8 * j + 8] for i in range(4)], axis=0
            ).astype(BF16)
            for i in range(2):
                corner = cells[6 * i + j]
                mcor[2 * i + j] = jnp.concatenate([corner, corner], axis=0).astype(BF16)

        def halo(row_first, row_last, col, cor, row_in, col_in, cor_in, sem):
            send(col.at[0], col_in.at[1], sem.at[3], (g, left_t))
            send(col.at[1], col_in.at[0], sem.at[2], (g, right_t))
            send(row_first, row_in.at[1], sem.at[1], (up_g, t))
            send(row_last, row_in.at[0], sem.at[0], (down_g, t))
            send(cor.at[0], cor_in.at[3], sem.at[7], (up_g, left_t))
            send(cor.at[1], cor_in.at[2], sem.at[6], (up_g, right_t))
            send(cor.at[2], cor_in.at[1], sem.at[5], (down_g, left_t))
            send(cor.at[3], cor_in.at[0], sem.at[4], (down_g, right_t))

        def halo_wait(row_in, col_in, cor_in, sem):
            for i in range(2):
                arrived(row_in.at[i], sem.at[i])
                arrived(col_in.at[i], sem.at[2 + i])
            for i in range(4):
                arrived(cor_in.at[i], sem.at[4 + i])

        halo(mrow.at[0], mrow.at[1], mcol, mcor, mrow_in, mcol_in, mcor_in, mh_sem)
        poll(POLLS[8])
        halo_wait(mrow_in, mcol_in, mcor_in, mh_sem)

        def surround(center, row_in, col_in, cor_in, height, breadth):
            lanes = row_in.shape[-1]

            def keep(values, *conditions):
                for condition in conditions:
                    values = jnp.where(inside(condition, values.shape), values, 0.0)
                return values

            above = keep(row_in[0].astype(F32), has_up).reshape(breadth, 8, lanes)
            below = keep(row_in[1].astype(F32), has_down).reshape(breadth, 8, lanes)
            left = keep(col_in[0].astype(F32), has_left).reshape(height, 8, lanes)
            right = keep(col_in[1].astype(F32), has_right).reshape(height, 8, lanes)
            corner = [
                keep(cor_in[2 * i + j].astype(F32)[0:8], (has_up, has_down)[i], (has_left, has_right)[j])
                for i in range(2)
                for j in range(2)
            ]
            tiles = [corner[0]] + [above[j] for j in range(breadth)] + [corner[1]]
            for i in range(height):
                tiles += [left[i]] + [center(i, j) for j in range(breadth)] + [right[i]]
            tiles += [corner[2]] + [below[j] for j in range(breadth)] + [corner[3]]
            return jnp.concatenate([tile[None] for tile in tiles], axis=0)

        low = surround(lambda i, j: cells[2 * i + j], mrow_in, mcol_in, mcor_in, 4, 2)
        around = activate(low)
        for a in range(3):
            moved = frames_back(around, 2 - a) if a < 2 else around
            moved = moved.reshape(192, 256).astype(BF16)
            for qh in range(2):
                mx3[:, pl.ds(384 * qh + 128 * a, 128)] = moved[:, 128 * qh : 128 * qh + 128]
        poll(len(events))

        for k in range(1, half_ring):
            arrived(block(sign * k, 0, 18), share_sem.at[k])
        arrived(block(half_ring, 9 * (1 - core), 9), share_sem.at[half_ring])

        def mid_tap(bc, _):
            filters = jnp.concatenate(
                [wm[:, bc + 9 * qh].reshape(256, 384) for qh in range(2)], axis=1
            )
            mprod[bc] = lax.dot_general(
                mx3[...], filters, NT_DIMS, preferred_element_type=F32
            ).reshape(6, 4, 8, 256)
            return 0

        lax.fori_loop(0, 9, mid_tap, 0, unroll=9)

        low = low.reshape(6, 4, 8, 256)
        for pr in range(2):
            for pc in range(2):
                total = low[1 - pr : 6 - pr, 1 - pc : 4 - pc]
                for b in range(3):
                    row = SHIFTS[pr][b] + 1 - pr
                    for c in range(3):
                        col = SHIFTS[pc][c] + 1 - pc
                        total = total + mprod[3 * b + c, pl.ds(row, 5), pl.ds(col, 3)]
                middle[pl.ds(120 * (2 * pr + pc), 120), :] = total.reshape(120, 256)
        fine_low = jnp.dot(middle[...].astype(BF16), mproj[...], preferred_element_type=F32)
        fine_low = fine_low.astype(BF16).astype(F32)
        lively = activate(fine_low)
        for pr in range(2):
            for pc in range(2):
                for i in range(5):
                    for j in range(3):
                        row, col = 2 * i + 1 - pr, 2 * j + 1 - pc
                        at = 120 * (2 * pr + pc) + 8 * (3 * i + j)
                        tile = lively[at : at + 8]
                        for edge, has in (
                            (row == 0, has_up), (row == 9, has_down),
                            (col == 0, has_left), (col == 5, has_right),
                        ):
                            if edge:
                                tile = jnp.where(inside(has, (8, 128)), tile, 0.0)
                        fx[row, col] = tile
                        if 1 <= row <= 8 and 1 <= col <= 4:
                            flow[row - 1, col - 1] = fine_low[at : at + 8]

        around = fx[...].reshape(60, 8, 128)
        fine = jnp.concatenate(
            [
                (frames_back(around, 2 - a) if a < 2 else around).reshape(480, 128).astype(BF16)
                for a in range(3)
            ],
            axis=1,
        )
        for pair in range(5):
            names = [bc for bc in (2 * pair, 2 * pair + 1) if bc < 9]
            filters = jnp.concatenate([fw[bc] for bc in names], axis=1)
            found = lax.dot_general(fine, filters, NN_DIMS, preferred_element_type=F32)
            for n, bc in enumerate(names):
                fprod[bc] = found[:, 128 * n : 128 * n + 128].reshape(10, 6, 8, 128)

        for pr in range(2):
            for pc in range(2):
                for i in range(8):
                    for j in range(4):
                        total = flow[i, j]
                        for b in range(3):
                            for c in range(3):
                                total = total + fprod[
                                    3 * b + c, i + 1 + SHIFTS[pr][b], j + 1 + SHIFTS[pc][c]
                                ]
                        spot = 8 * (2 * i + pr) + 2 * j + pc
                        result[pl.ds(spot, 8, stride=128), :] = total
        out[...] = result[...].astype(BF16).reshape(8, 16, 8, 128)

        for copy in sent:
            copy.wait_send()

    return kernel


def count_sends(nz):
    return 6 + 24 + 1 + 4 * (nz // 2) + 2 + 15 + 8


def body(latent, coarse_filters, mid_filters, fine_filters, coarse_proj, mid_proj):
    nz = lax.axis_size("tile") // 2
    outs = mid_filters.shape[4]
    cw = jnp.transpose(coarse_filters, (0, 1, 2, 4, 3)).reshape(3, 9, 32, 512)
    mw = jnp.transpose(mid_filters, (0, 1, 2, 4, 3)).reshape(27, outs, 256)
    fw = fine_filters.reshape(3, 9, 128, 128)
    vmem = pl.BlockSpec(memory_space=pltpu.VMEM)
    half = nz // 2
    dma = pltpu.SemaphoreType.DMA
    return pl.pallas_call(
        make_kernel(nz),
        out_shape=jax.ShapeDtypeStruct((8, 16, 8, 128), BF16),
        in_specs=[pl.BlockSpec(memory_space=pl.ANY)] * 6,
        out_specs=vmem,
        scratch_shapes=[
            pltpu.VMEM((8, 4, 2, 512), BF16),
            pltpu.VMEM((27, outs, 256), BF16),
            pltpu.VMEM((512, 256), BF16),
            pltpu.VMEM((256, 128), BF16),
            pltpu.VMEM((4, 64, 128), F32),
            pltpu.VMEM((16, 64, 512), BF16),
            pltpu.VMEM((9, 128, 512), BF16),
            pltpu.VMEM((9, 66, 16, 128), F32),
            pltpu.VMEM((2, 8, 16, 128), BF16),
            pltpu.VMEM((2, 8, 16, 128), BF16),
            pltpu.VMEM((16, 16, 128), F32),
            pltpu.VMEM((16, 16, 128), BF16),
            pltpu.VMEM((16, 16, 128), BF16),
            pltpu.VMEM((28 * outs, 256), BF16),
            pltpu.VMEM((28 * outs, 256), BF16),
            pltpu.VMEM((nz, 18, 2 * outs, 384), BF16),
            pltpu.VMEM((64, 512), BF16),
            pltpu.VMEM((2, 16, 256), BF16),
            pltpu.VMEM((2, 32, 256), BF16),
            pltpu.VMEM((4, 16, 256), BF16),
            pltpu.VMEM((2, 16, 256), BF16),
            pltpu.VMEM((2, 32, 256), BF16),
            pltpu.VMEM((4, 16, 256), BF16),
            pltpu.VMEM((192, 768), BF16),
            pltpu.VMEM((9, 6, 4, 8, 256), F32),
            pltpu.VMEM((480, 256), F32),
            pltpu.VMEM((9, 384, 128), BF16),
            pltpu.VMEM((8, 4, 8, 128), F32),
            pltpu.VMEM((10, 6, 8, 128), F32),
            pltpu.VMEM((9, 10, 6, 8, 128), F32),
            pltpu.VMEM((1024, 128), F32),
            dma((10,)),
            dma((count_sends(nz),)),
            dma((2, 3)),
            dma((2, 4, 3)),
            dma((1,)),
            dma((half + 1, 3)),
            dma((half + 1,)),
            dma((2,)),
            dma((16,)),
            dma((8,)),
        ],
        compiler_params=pltpu.CompilerParams(
            collective_id=0, has_side_effects=True, vmem_limit_bytes=60 * 1024 * 1024
        ),
    )(latent, cw, mw, fw, coarse_proj, mid_proj)


def solution(mesh):
    in_specs = (
        P(None, "grp", "tile", None),
        P(None, None, None, None, "grp"),
        P(None, None, None, None, "tile"),
        P(),
        P(),
        P(),
    )
    out_specs = P(None, "grp", "tile", None)
    return jax.shard_map(body, mesh=mesh, in_specs=in_specs, out_specs=out_specs, check_vma=False)
```
